128 devices in a mesh: chain: 8 (over y, z_hi), resp: 16 (over x, z_lo, core).
Axes of the slice: x: 4, y: 4, z: 4 (z_hi: 2, z_lo: 2; z = z_hi * 2 + z_lo), core: 2. Of those that a mesh axis runs over, the one named last changes fastest.
Arguments:
- q_prompt: bfloat16 [4096, 8192], P('chain', 'resp'), may hold values from -8 to 8
- k_prompt: bfloat16 [4096, 1024], P(('chain', 'resp')), may hold values from -8 to 8
- v_prompt: bfloat16 [4096, 1024], P(('chain', 'resp')), may hold values from -6 to 6
- q_resp: bfloat16 [16, 512, 8192], P('resp', None, 'chain'), may hold values from -8 to 8
- k_resp: bfloat16 [16, 512, 1024], P('resp', None, 'chain'), may hold values from -6 to 6
- v_resp: bfloat16 [16, 512, 1024], P('resp', None, 'chain'), may hold values from -6 to 6
- tree_table: int32 [16, 8], P('resp'), may hold values from -1 to 6, as said below
- lengths: int32 [16], P('resp'), may hold values from 256 to 512, as said below
Outputs:
- prompt_out: bfloat16 [4096, 8192], P('chain', 'resp')
- resp_out: bfloat16 [16, 512, 8192], P('resp', None, 'chain')
The draws below stay inside these ranges and needn't reach their ends.
Inputs may be any that keep to these rules, and one draw needn't show every extreme that they name: `tree_table`: entry j of a response's row is -1 (the block has no parent) or the index of an earlier block of that response; entry 0 is -1. `lengths`: some response has 512 live tokens.
All inputs are finite; a program needn't handle non-finite values.
Results may differ from the reference program's by a relative error of at most 0.009.
Values may be sent and summed in bfloat16 or wider, within the bound.
No kernel may reach another device: no remote copies, remote signals or barrier semaphores. Data moves between devices by JAX's collectives and lax.ppermute only.
A program may use at most 64 MiB of HBM per device.

```python
import jax
import jax.numpy as jnp
from jax import lax

QH = 64
KVH = 8
HD = 128
RLEN = 512
RBLK = 8
PROMPT = 4096
NRESP = 16


def draw_q_prompt(key, part):
    key = jax.random.fold_in(key, 1)
    values = jax.random.truncated_normal(key, -4.0, 4.0, (PROMPT, QH * HD), jnp.float32)
    return values.astype(jnp.bfloat16)


def draw_k_prompt(key, part):
    key = jax.random.fold_in(key, 2)
    values = jax.random.truncated_normal(key, -4.0, 4.0, (PROMPT, KVH * HD), jnp.float32)
    return values.astype(jnp.bfloat16)


def draw_q_resp(key, part):
    key = jax.random.fold_in(key, 3)
    values = jax.random.truncated_normal(key, -4.0, 4.0, (NRESP, RLEN, QH * HD), jnp.float32)
    return values.astype(jnp.bfloat16)


def draw_tree_table(key, part):
    key = jax.random.fold_in(key, 6)
    first, second = jax.random.split(key)
    parents = jax.random.randint(first, (NRESP, RBLK), -1, jnp.arange(RBLK, dtype=jnp.int32))
    which_row = jax.random.randint(second, (), 0, NRESP)
    return parents.at[which_row, RBLK - 1].set(RBLK - 2).astype(jnp.int32)


def draw_lengths(key, part):
    key = jax.random.fold_in(key, 5)
    first, second, third = jax.random.split(key, 3)
    values = jax.random.randint(first, (NRESP,), RLEN // 2, RLEN + 1)
    full_at = jax.random.randint(second, (), 0, NRESP)
    half_at = (full_at + 1 + jax.random.randint(third, (), 0, NRESP - 1)) % NRESP
    values = values.at[full_at].set(RLEN).at[half_at].set(RLEN // 2)
    return values.astype(jnp.int32)


def levels(key, dims, pieces, smallest, largest):
    level = 1.0
    for dim, parts in pieces:
        draws = jax.random.uniform(jax.random.fold_in(jax.random.fold_in(key, 6), dim), (parts,), jnp.float32, smallest / len(pieces), largest / len(pieces))
        level = level * jnp.repeat(jnp.exp(draws), dims[dim] // parts).reshape((-1,) + (1,) * (len(dims) - 1 - dim))
    return level


def noise(stream_key, extent, scale, most, cuts=(), kind=jnp.bfloat16):
    result = scale * jax.random.normal(stream_key, extent, jnp.float32)
    if cuts:
        result = result * levels(stream_key, extent, cuts, -0.22, 0.18)
    return jnp.clip(result, -most, most).astype(kind)


def setup_inputs(seed: int = 0) -> dict:
    splits = jax.random.split(jax.random.key(seed), 9)
    return {
        "q_prompt": draw_q_prompt(jax.random.fold_in(splits[8], 71), 0),
        "k_prompt": draw_k_prompt(jax.random.fold_in(splits[8], 71), 0),
        "v_prompt": noise(splits[2], (PROMPT, KVH * HD), 1.0, 6.0, ((0, 128),)),
        "q_resp": draw_q_resp(jax.random.fold_in(splits[8], 71), 0),
        "k_resp": noise(splits[4], (NRESP, RLEN, KVH * HD), 1.0, 6.0, ((0, 16), (2, 8))),
        "v_resp": noise(splits[5], (NRESP, RLEN, KVH * HD), 1.0, 6.0, ((0, 16), (2, 8))),
        "tree_table": draw_tree_table(jax.random.fold_in(splits[8], 71), 0),
        "lengths": draw_lengths(jax.random.fold_in(splits[8], 71), 0),
    }


def tree_visible(parent, live_len, row_count, blocks):
    span_rows = row_count // blocks
    block_ids = jnp.arange(blocks, dtype=jnp.int32)
    parent_hot = (parent[:, None] == block_ids[None, :]).astype(jnp.float32)
    ancestry = jnp.eye(blocks, dtype=jnp.float32)
    for which_block in range(blocks):
        upward = jnp.dot(parent_hot[which_block], ancestry, precision=lax.Precision.HIGHEST)
        ancestry = ancestry.at[which_block].set(ancestry[which_block] + upward)
    wide = jnp.repeat(jnp.repeat(ancestry, span_rows, 0), span_rows, 1) > 0.5
    places = jnp.arange(row_count, dtype=jnp.int32)
    return wide & (places[None, :] <= places[:, None]) & (places[None, :] < live_len)


def attend(queries, key_rows, value_rows, visible):
    factor = HD ** -0.5
    scores = jnp.dot(queries, key_rows.T, preferred_element_type=jnp.float32) * factor
    capped = jnp.where(visible, scores, -1e30)
    row_max = jnp.max(capped, axis=-1, keepdims=True)
    weights = jnp.where(visible, jnp.exp(scores - row_max), 0.0)
    totals = jnp.sum(weights, axis=-1, keepdims=True)
    weighted = jnp.dot(weights.astype(jnp.bfloat16), value_rows, preferred_element_type=jnp.float32)
    return weighted / totals


def reference(q_prompt, k_prompt, v_prompt, q_resp, k_resp, v_resp, tree_table, lengths):
    group_size = QH // KVH
    q_heads = q_prompt.reshape(PROMPT, QH, HD).transpose(1, 0, 2)
    k_heads = k_prompt.reshape(PROMPT, KVH, HD).transpose(1, 0, 2)
    v_heads = v_prompt.reshape(PROMPT, KVH, HD).transpose(1, 0, 2)
    places = jnp.arange(PROMPT, dtype=jnp.int32)
    causal = places[:, None] >= places[None, :]

    def prompt_head(head_index):
        queries = lax.dynamic_index_in_dim(q_heads, head_index, 0, False)
        key_rows = lax.dynamic_index_in_dim(k_heads, head_index // group_size, 0, False)
        value_rows = lax.dynamic_index_in_dim(v_heads, head_index // group_size, 0, False)
        return attend(queries, key_rows, value_rows, causal)

    prompt_heads = lax.map(prompt_head, jnp.arange(QH, dtype=jnp.int32))
    prompt_out = prompt_heads.transpose(1, 0, 2).reshape(PROMPT, QH * HD).astype(jnp.bfloat16)

    def one_response(inputs):
        resp_queries, resp_keys, resp_values, parent, live_len = inputs
        own_visible = tree_visible(parent, live_len, RLEN, RBLK)
        visible = jnp.concatenate([jnp.ones((RLEN, PROMPT), dtype=bool), own_visible], axis=1)
        all_keys = jnp.concatenate([k_prompt.reshape(PROMPT, KVH, HD), resp_keys.reshape(RLEN, KVH, HD)], 0).transpose(1, 0, 2)
        all_values = jnp.concatenate([v_prompt.reshape(PROMPT, KVH, HD), resp_values.reshape(RLEN, KVH, HD)], 0).transpose(1, 0, 2)
        query_heads = resp_queries.reshape(RLEN, QH, HD).transpose(1, 0, 2)

        def resp_head(head_index):
            queries = lax.dynamic_index_in_dim(query_heads, head_index, 0, False)
            key_rows = lax.dynamic_index_in_dim(all_keys, head_index // group_size, 0, False)
            value_rows = lax.dynamic_index_in_dim(all_values, head_index // group_size, 0, False)
            return attend(queries, key_rows, value_rows, visible)

        heads_out = lax.map(resp_head, jnp.arange(QH, dtype=jnp.int32))
        joined = heads_out.transpose(1, 0, 2).reshape(RLEN, QH * HD)
        live_rows = jnp.arange(RLEN, dtype=jnp.int32) < live_len
        return jnp.where(live_rows[:, None], joined, 0.0).astype(jnp.bfloat16)

    resp_out = lax.map(one_response, (q_resp, k_resp, v_resp, tree_table, lengths))
    return prompt_out, resp_out
```

```python
import functools

import jax
import jax.numpy as jnp
from jax import lax
from jax.experimental import pallas as pl
from jax.experimental.pallas import tpu as pltpu
from jax.sharding import PartitionSpec as P

QH = 64
KVH = 8
HD = 128
RBLK = 8
ROWS = 512
SUB = 32
GROUP = QH // KVH
SCALE = HD**-0.5 * 1.4426950408889634
LOW, HIGH = 1e-18, 1e30
AXES = ("chain", "resp")
STEPS = (0, 1, 3, 2)
MIB = 2**20
PLACES = [(y, z, x, k) for y in range(4) for z in range(4) for x in range(4) for k in range(2)]


def device_at(y, z, x, core):
    return (y * 2 + z // 2) * 16 + (x * 2 + z % 2) * 2 + core


def move(block, target):
    route = [(device_at(*p), device_at(*target(*p))) for p in PLACES]
    return lax.ppermute(block, AXES, route)


def move_back(block, target):
    route = [(device_at(*target(*p)), device_at(*p)) for p in PLACES]
    return lax.ppermute(block, AXES, route)


def along_y(d):
    return lambda y, z, x, core: ((y + d) % 4, z, x, core)


def along_z(d):
    return lambda y, z, x, core: (y, (z + d) % 4, x, core)


def along_x(d):
    return lambda y, z, x, core: (y, z, (x + d) % 4, core)


def other_core(y, z, x, core):
    return (y, z, x, 1 - core)


def query_home(half):
    def target(y, z, x, core):
        hi, lo = z // 2, z % 2
        if half:
            y, hi = 3 - y, 1 - hi
        return (x, lo * 2 + hi, (y + x) % 4, core)

    return target


def dot_t(a, b):
    return lax.dot_general(a, b, (((1,), (1,)), ((), ())), preferred_element_type=jnp.float32)


def fold_rows(p):
    return jnp.sum(p.reshape(p.shape[0] // 8, 8, p.shape[1]), axis=0)


def token_rows(block):
    return block.reshape(-1, HD)


def online(carried, keys, values_t, queries, visible):
    run_max, run_sum, run_acc = carried
    scores = dot_t(keys, queries) * SCALE
    if visible is not None:
        scores = jnp.where(visible, scores, -1e30)
    new_max = jnp.maximum(run_max, jnp.max(scores, axis=0, keepdims=True))
    weights = jnp.exp2(scores - new_max)
    if visible is not None:
        weights = jnp.where(visible, weights, 0.0)
    rescale = jnp.exp2(run_max - new_max)
    run_sum = run_sum * rescale + jnp.sum(weights, axis=0, keepdims=True)
    added = jnp.dot(values_t, weights.astype(jnp.bfloat16), preferred_element_type=jnp.float32)
    return (new_max, run_sum, run_acc * rescale + added)


def fresh(cols):
    return (
        jnp.full((1, cols), -1e30, jnp.float32),
        jnp.zeros((1, cols), jnp.float32),
        jnp.zeros((HD, cols), jnp.float32),
    )


def tree_seen(tree_ref, len_ref):
    lines = []
    for j in range(RBLK):
        parent = tree_ref[0, j]
        line = jnp.int32(1 << j)
        for i in range(j):
            line = line | jnp.where(parent == i, lines[i], 0)
        lines.append(line)
    key_at = lax.broadcasted_iota(jnp.int32, (ROWS, ROWS), 0)
    row_at = lax.broadcasted_iota(jnp.int32, (ROWS, ROWS), 1)
    span = ROWS // RBLK
    line_of_row = jnp.zeros((ROWS, ROWS), jnp.int32)
    for j in range(RBLK):
        line_of_row = jnp.where(row_at // span == j, lines[j], line_of_row)
    related = (lax.shift_right_logical(line_of_row, key_at // span) & 1) == 1
    return related & (key_at <= row_at) & (key_at < len_ref[0])


def own_kernel(tree_ref, len_ref, q_ref, k_ref, v_ref, acc_ref, sum_ref, seen, vt):
    @pl.when(pl.program_id(0) == 0)
    def _():
        seen[...] = jnp.where(tree_seen(tree_ref, len_ref), 0.0, -jnp.inf)
        vt[...] = v_ref[...].T

    weights = jnp.exp2(dot_t(k_ref[...], q_ref[...]) * SCALE + seen[...])
    sum_ref[0] = fold_rows(weights)
    acc_ref[0] = jnp.dot(vt[...], weights.astype(jnp.bfloat16), preferred_element_type=jnp.float32)


def load_chunks(parts, kb, vt):
    at = 0
    for part in parts:
        keys, values = token_rows(part[:, 0]), token_rows(part[:, 1])
        count = keys.shape[0]
        kb[at : at + count, :] = keys
        vt[:, at : at + count] = values.T
        at += count


def chunk_kernel(part_count, *refs):
    q_ref, acc_in, sum_in = refs[:3]
    parts = refs[3 : 3 + part_count]
    acc_ref, sum_ref, kb, vt = refs[3 + part_count :]

    @pl.when(pl.program_id(0) == 0)
    def _():
        load_chunks(parts, kb, vt)

    weights = jnp.exp2(dot_t(kb[...], q_ref[...]) * SCALE)
    sum_ref[0] = sum_in[0] + fold_rows(weights)
    acc_ref[0] = acc_in[0] + jnp.dot(
        vt[...], weights.astype(jnp.bfloat16), preferred_element_type=jnp.float32
    )


def last_kernel(part_count, slabs, *refs):
    tree_ref, len_ref, q_ref, acc_in, sum_in = refs[:5]
    parts = refs[5 : 5 + part_count]
    refs = refs[5 + part_count :]
    q_all, k_own, v_own = refs[:3]
    held = refs[3 : 3 + len(slabs)]
    out_ref, kb, vt, low, high, slab, q_buf, own_buf = refs[3 + len(slabs) :]
    head = pl.program_id(0)

    @pl.when(head == 0)
    def _():
        load_chunks(parts, kb, vt)
        low[...] = jnp.full_like(low, 1.0)
        high[...] = jnp.full_like(high, 1.0)

    live = lax.broadcasted_iota(jnp.int32, (ROWS, HD), 0) < len_ref[0]
    weights = jnp.exp2(dot_t(kb[...], q_ref[...]) * SCALE)
    total = jnp.sum(sum_in[0] + fold_rows(weights), axis=0, keepdims=True)
    acc = acc_in[0] + jnp.dot(
        vt[...], weights.astype(jnp.bfloat16), preferred_element_type=jnp.float32
    )
    low[...] = jnp.minimum(low[...], total)
    high[...] = jnp.maximum(high[...], total)
    cols = pl.ds(pl.multiple_of(head * HD, HD), HD)
    out_ref[:, cols] = jnp.where(live, (acc / total).T, 0.0).astype(jnp.bfloat16)

    @pl.when(head == pl.num_programs(0) - 1)
    def _():
        good = (jnp.min(low[...]) > LOW) & (jnp.max(high[...]) < HIGH)

        @pl.when(jnp.logical_not(good))
        def _():
            pltpu.sync_copy(k_own, own_buf.at[0])
            pltpu.sync_copy(v_own, own_buf.at[1])

            def one_head(h, unused):
                at = pl.multiple_of(h * HD, HD)
                pltpu.sync_copy(q_all.at[:, pl.ds(at, HD)], q_buf)
                queries = q_buf[...]
                carried = fresh(ROWS)
                for ref, spots in zip(held, slabs):
                    for spot in range(spots):
                        pltpu.sync_copy(ref.at[pl.ds(spot * 16, 16)], slab)
                        carried = online(
                            carried, token_rows(slab[:, 0]), token_rows(slab[:, 1]).T, queries, None
                        )
                seen = tree_seen(tree_ref, len_ref)
                run_max, run_sum, run_acc = online(
                    carried, own_buf[0], own_buf[1].T, queries, seen
                )
                shown = jnp.where(live, (run_acc / run_sum).T, 0.0)
                out_ref[:, pl.ds(at, HD)] = shown.astype(jnp.bfloat16)
                return unused

            lax.fori_loop(0, GROUP, one_head, 0)


def prompt_kernel(place_ref, qa_ref, qb_ref, *refs):
    here, here_s, wide, wide_s, far, far_s = refs[:6]
    outs = refs[6:8]
    kb, vb, vt, qs, acc, total = refs[8:]
    y, z, x, core = (place_ref[i] for i in range(4))
    half = ROWS // 2
    heads = GROUP // 2
    wide_cols = heads * half

    def place(ref, at, z_step, y_step, x_from, core_from):
        y0 = (y - y_step) % 4
        z0 = (z - z_step) % 4
        block = (y0 * 2 + z0 // 2) * 16 + (x_from * 2 + z0 % 2) * 2 + core_from
        spot = pl.ds(pl.multiple_of(block * SUB, SUB), SUB)
        kb[spot, :] = ref[at, 0]
        vb[spot, :] = ref[at, 1]

    for ref, wide_ref, far_ref, core_from in (
        (here, wide, far, core),
        (here_s, wide_s, far_s, 1 - core),
    ):
        for i, z_step in enumerate(STEPS):
            for j, y_step in enumerate(STEPS):
                at = i * 4 + j
                place(ref, at, z_step, y_step, x, core_from)
                place(wide_ref, at, z_step, y_step, (x + 3) % 4, core_from)
                place(wide_ref, 16 + at, z_step, y_step, (x + 1) % 4, core_from)
                place(far_ref, at, z_step, y_step, (x + 2) % 4, core_from)
    for b in range(8):
        vt[b] = vb[b * ROWS : (b + 1) * ROWS, :].T
    for side, q_ref in enumerate((qa_ref, qb_ref)):
        for h in range(heads):
            qs[side, h * half : (h + 1) * half, :] = q_ref[:, h * HD : (h + 1) * HD]

    block_a = ((x - y) % 4) * 2 + z % 2
    blocks = (block_a, 7 - block_a)

    def key_rows(block, count):
        return kb[pl.ds(pl.multiple_of(block * ROWS, ROWS), count), :]

    for side, count in ((0, half), (1, ROWS)):
        scores = dot_t(key_rows(blocks[side], count), qs[side]) * SCALE
        key_at = lax.broadcasted_iota(jnp.int32, scores.shape, 0)
        row_at = lax.broadcasted_iota(jnp.int32, scores.shape, 1) % half + side * half
        weights = jnp.where(key_at <= row_at, jnp.exp2(scores), 0.0)
        total[side] = fold_rows(weights)
        acc[side] = jnp.dot(
            vt[blocks[side]][:, :count],
            weights.astype(jnp.bfloat16),
            preferred_element_type=jnp.float32,
        )
    for n in range(7):
        first = n < block_a
        side = jnp.where(first, 0, 1)
        block = jnp.where(first, n, n - block_a)
        weights = jnp.exp2(dot_t(key_rows(block, ROWS), qs[side]) * SCALE)
        total[side] += fold_rows(weights)
        acc[side] += jnp.dot(
            vt[block], weights.astype(jnp.bfloat16), preferred_element_type=jnp.float32
        )

    def store(side, sums, accs):
        shown = accs / sums
        for h in range(heads):
            outs[side][:, h * HD : (h + 1) * HD] = shown[:, h * half : (h + 1) * half].T.astype(
                jnp.bfloat16
            )

    sums = [jnp.sum(total[side], axis=0, keepdims=True) for side in range(2)]
    for side in range(2):
        store(side, sums[side], acc[side])
    least = jnp.min(jnp.minimum(sums[0], sums[1]))
    most = jnp.max(jnp.maximum(sums[0], sums[1]))
    good = (least > LOW) & (most < HIGH)

    @pl.when(jnp.logical_not(good))
    def _():
        for side in range(2):

            def one_block(b, carried, side=side):
                key_at = lax.broadcasted_iota(jnp.int32, (ROWS, wide_cols), 0) + b * ROWS
                row_at = lax.broadcasted_iota(jnp.int32, (ROWS, wide_cols), 1) % half
                row_at = row_at + side * half + blocks[side] * ROWS
                return online(carried, key_rows(b, ROWS), vt[b], qs[side], key_at <= row_at)

            run_max, run_sum, run_acc = lax.fori_loop(
                0, blocks[side] + 1, one_block, fresh(wide_cols)
            )
            store(side, run_sum, run_acc)


def whole(shape):
    return pl.BlockSpec(shape, lambda h: (0,) * len(shape))


STATE = (
    jax.ShapeDtypeStruct((GROUP, HD, ROWS), jnp.float32),
    jax.ShapeDtypeStruct((GROUP, 8, ROWS), jnp.float32),
)
STATE_SPECS = (
    pl.BlockSpec((1, HD, ROWS), lambda h: (h, 0, 0)),
    pl.BlockSpec((1, 8, ROWS), lambda h: (h, 0, 0)),
)
HEAD_SPEC = pl.BlockSpec((ROWS, HD), lambda h: (0, h))
SCALAR = pl.BlockSpec(memory_space=pltpu.SMEM)
PARAMS = dict(compiler_params=pltpu.CompilerParams(vmem_limit_bytes=48 * MIB))


def cost(rows, keys):
    return pl.CostEstimate(
        flops=8 * rows * keys * HD, bytes_accessed=6 * MIB, transcendentals=rows * keys
    )


def attend_own(tree, length, q, k, v):
    return pl.pallas_call(
        own_kernel,
        grid=(GROUP,),
        in_specs=[SCALAR, SCALAR, HEAD_SPEC, whole((ROWS, HD)), whole((ROWS, HD))],
        out_specs=STATE_SPECS,
        out_shape=STATE,
        scratch_shapes=[
            pltpu.VMEM((ROWS, ROWS), jnp.float32),
            pltpu.VMEM((HD, ROWS), jnp.bfloat16),
        ],
        cost_estimate=cost(GROUP * ROWS, ROWS),
        name="own_keys",
        **PARAMS,
    )(tree, length, q, k, v)


def attend_chunk(q, state, parts, name):
    tokens = sum(part.shape[0] for part in parts) * SUB
    return pl.pallas_call(
        functools.partial(chunk_kernel, len(parts)),
        grid=(GROUP,),
        in_specs=[HEAD_SPEC, *STATE_SPECS] + [whole(part.shape) for part in parts],
        out_specs=STATE_SPECS,
        out_shape=STATE,
        scratch_shapes=[
            pltpu.VMEM((tokens, HD), jnp.bfloat16),
            pltpu.VMEM((HD, tokens), jnp.bfloat16),
        ],
        cost_estimate=cost(GROUP * ROWS, tokens),
        name=name,
        **PARAMS,
    )(q, *state, *parts)


def attend_last(tree, length, q, state, parts, k_own, v_own, held):
    tokens = sum(part.shape[0] for part in parts) * SUB
    slabs = tuple(part.shape[0] // 16 for part in held)
    anywhere = pl.BlockSpec(memory_space=pl.ANY)
    return pl.pallas_call(
        functools.partial(last_kernel, len(parts), slabs),
        grid=(GROUP,),
        in_specs=[SCALAR, SCALAR, HEAD_SPEC, *STATE_SPECS]
        + [whole(part.shape) for part in parts]
        + [anywhere] * (3 + len(held)),
        out_specs=whole((ROWS, GROUP * HD)),
        out_shape=jax.ShapeDtypeStruct((ROWS, GROUP * HD), jnp.bfloat16),
        scratch_shapes=[
            pltpu.VMEM((tokens, HD), jnp.bfloat16),
            pltpu.VMEM((HD, tokens), jnp.bfloat16),
            pltpu.VMEM((1, ROWS), jnp.float32),
            pltpu.VMEM((1, ROWS), jnp.float32),
            pltpu.VMEM((16, 2, SUB, HD), jnp.bfloat16),
            pltpu.VMEM((ROWS, HD), jnp.bfloat16),
            pltpu.VMEM((2, ROWS, HD), jnp.bfloat16),
        ],
        cost_estimate=cost(GROUP * ROWS, tokens),
        name="last_keys",
        **PARAMS,
    )(tree, length, q, *state, *parts, q, k_own, v_own, *held)


def attend_prompt(place, qa, qb, held):
    half = ROWS // 2
    vmem = pl.BlockSpec(memory_space=pltpu.VMEM)
    cols = GROUP // 2 * half
    return pl.pallas_call(
        prompt_kernel,
        in_specs=[SCALAR] + [vmem] * (2 + len(held)),
        out_specs=[vmem, vmem],
        out_shape=[jax.ShapeDtypeStruct(qa.shape, jnp.bfloat16)] * 2,
        scratch_shapes=[
            pltpu.VMEM((8 * ROWS, HD), jnp.bfloat16),
            pltpu.VMEM((8 * ROWS, HD), jnp.bfloat16),
            pltpu.VMEM((8, HD, ROWS), jnp.bfloat16),
            pltpu.VMEM((2, cols, HD), jnp.bfloat16),
            pltpu.VMEM((2, HD, cols), jnp.float32),
            pltpu.VMEM((2, 8, cols), jnp.float32),
        ],
        cost_estimate=cost(cols, 9 * ROWS),
        name="prompt_rows",
        **PARAMS,
    )(place, qa, qb, *held)


def pick(block, index, axis=0):
    return lax.dynamic_index_in_dim(block, index, axis, False)


def on_device(q_prompt, k_prompt, v_prompt, q_resp, k_resp, v_resp, tree_table, lengths):
    chain, resp = lax.axis_index("chain"), lax.axis_index("resp")
    y, z, x, core = chain // 2, chain % 2 * 2 + resp // 2 % 2, resp // 4, resp % 2
    place = jnp.stack([y, z, x, core]).astype(jnp.int32)
    half = ROWS // 2
    q = q_resp[0]

    pieces = jnp.stack([k_prompt.reshape(SUB, KVH, HD), v_prompt.reshape(SUB, KVH, HD)])
    pieces = pieces.transpose(2, 0, 1, 3).reshape(4, 2, 2, SUB, HD)
    over_y = [pick(pieces, y)]
    over_y += [move(pick(pieces, (y + d) % 4), along_y(d)) for d in STEPS[1:]]
    over_y = jnp.stack(over_y)
    over_z = [pick(over_y, z // 2, 1)]
    over_z += [move(pick(over_y, (z + d) % 4 // 2, 1), along_z(d)) for d in STEPS[1:]]
    here = jnp.concatenate(over_z)
    here_s = move(here, other_core)
    from_left, from_right = move(here, along_x(1)), move(here, along_x(3))
    wide = jnp.concatenate([from_left, from_right])
    wide_s = move(wide, other_core)
    far = jnp.concatenate([move(from_left[:8], along_x(1)), move(from_right[8:], along_x(3))])
    far_s = move(far, other_core)

    qa = move(q_prompt[:half], query_home(0))
    qb = move(q_prompt[half:], query_home(1))

    state = attend_own(tree_table, lengths, q, k_resp[0], v_resp[0])
    state = attend_chunk(q, state, (here, here_s), "here_keys")
    held = (here, here_s, wide, wide_s, far, far_s)
    out_a, out_b = attend_prompt(place, qa, qb, held)
    out_a = move_back(out_a, query_home(0))
    out_b = move_back(out_b, query_home(1))
    prompt_out = jnp.concatenate([out_a, out_b])
    state = attend_chunk(q, state, (wide, wide_s), "wide_keys")
    resp_out = attend_last(
        tree_table, lengths, q, state, (far, far_s), k_resp[0], v_resp[0], held
    )
    return (prompt_out, resp_out[None])


def solution(mesh):
    placed = (
        P("chain", "resp"),
        P(("chain", "resp"), None),
        P(("chain", "resp"), None),
        P("resp", None, "chain"),
        P("resp", None, "chain"),
        P("resp", None, "chain"),
        P("resp", None),
        P("resp"),
    )
    return jax.shard_map(
        on_device,
        mesh=mesh,
        in_specs=placed,
        out_specs=(P("chain", "resp"), P("resp", None, "chain")),
        check_vma=False,
    )
```

```python
import functools

import jax
import jax.numpy as jnp
from jax import lax
from jax.experimental import pallas as pl
from jax.experimental.pallas import tpu as pltpu
from jax.sharding import PartitionSpec as P

QH = 64
KVH = 8
HD = 128
RBLK = 8
ROWS = 512
SUB = 32
GROUP = QH // KVH
STEP_HEADS = 4
SCALE = HD**-0.5 * 1.4426950408889634
LOW, HIGH = 1e-18, 1e30
AXES = ("chain", "resp")
STEPS = (0, 1, 3, 2)
MIB = 2**20
PLACES = [(y, z, x, k) for y in range(4) for z in range(4) for x in range(4) for k in range(2)]


def device_at(y, z, x, core):
    return (y * 2 + z // 2) * 16 + (x * 2 + z % 2) * 2 + core


def move(block, target):
    route = [(device_at(*p), device_at(*target(*p))) for p in PLACES]
    return lax.ppermute(block, AXES, route)


def along_y(d):
    return lambda y, z, x, core: ((y + d) % 4, z, x, core)


def along_z(d):
    return lambda y, z, x, core: (y, (z + d) % 4, x, core)


def other_core(y, z, x, core):
    return (y, z, x, 1 - core)


def along_x(d):
    return lambda y, z, x, core: (y, z, (x + d) % 4, core)


def both_ways_x(y, z, x, core):
    return (y, z, (x + 1 + 2 * core) % 4, core)


def both_ways_y(y, z, x, core):
    return ((y + 1 + 2 * core) % 4, z, x, core)


def dot_t(a, b):
    return lax.dot_general(a, b, (((1,), (1,)), ((), ())), preferred_element_type=jnp.float32)


def fold_rows(p):
    return jnp.sum(p.reshape(p.shape[0] // 8, 8, p.shape[1]), axis=0)


def token_rows(block):
    return block.reshape(-1, HD)


def online(carried, keys, values_t, queries, visible):
    run_max, run_sum, run_acc = carried
    scores = dot_t(keys, queries) * SCALE
    if visible is not None:
        scores = jnp.where(visible, scores, -1e30)
    new_max = jnp.maximum(run_max, jnp.max(scores, axis=0, keepdims=True))
    weights = jnp.exp2(scores - new_max)
    if visible is not None:
        weights = jnp.where(visible, weights, 0.0)
    rescale = jnp.exp2(run_max - new_max)
    run_sum = run_sum * rescale + jnp.sum(weights, axis=0, keepdims=True)
    added = jnp.dot(values_t, weights.astype(jnp.bfloat16), preferred_element_type=jnp.float32)
    return (new_max, run_sum, run_acc * rescale + added)


def fresh(cols):
    return (
        jnp.full((1, cols), -1e30, jnp.float32),
        jnp.zeros((1, cols), jnp.float32),
        jnp.zeros((HD, cols), jnp.float32),
    )


def tree_seen(tree_ref, len_ref):
    lines = []
    for j in range(RBLK):
        parent = tree_ref[0, j]
        line = jnp.int32(1 << j)
        for i in range(j):
            line = line | jnp.where(parent == i, lines[i], 0)
        lines.append(line)
    key_at = lax.broadcasted_iota(jnp.int32, (ROWS, ROWS), 0)
    row_at = lax.broadcasted_iota(jnp.int32, (ROWS, ROWS), 1)
    span = ROWS // RBLK
    line_of_row = jnp.zeros((ROWS, ROWS), jnp.int32)
    for j in range(RBLK):
        line_of_row = jnp.where(row_at // span == j, lines[j], line_of_row)
    related = (lax.shift_right_logical(line_of_row, key_at // span) & 1) == 1
    return related & (key_at <= row_at) & (key_at < len_ref[0])


def load_chunks(parts, kb, vt):
    at = 0
    for part in parts:
        keys, values = token_rows(part[:, 0]), token_rows(part[:, 1])
        count = keys.shape[0]
        kb[at : at + count, :] = keys
        vt[:, at : at + count] = values.T
        at += count


def weigh(keys, queries, values_t, shown=None):
    scores = dot_t(keys, queries) * SCALE
    weights = jnp.exp2(scores if shown is None else scores + shown)
    added = jnp.dot(values_t, weights.astype(jnp.bfloat16), preferred_element_type=jnp.float32)
    return fold_rows(weights), added


def first_kernel(part_count, tree_ref, len_ref, q_ref, k_own, v_own, *refs):
    parts = refs[:part_count]
    acc_ref, sum_ref, kb, vt, vt_own, seen = refs[part_count:]

    @pl.when(pl.program_id(0) == 0)
    def _():
        load_chunks(parts, kb, vt)
        vt_own[...] = v_own[...].T
        seen[...] = jnp.where(tree_seen(tree_ref, len_ref), 0.0, -jnp.inf)

    for h in range(STEP_HEADS):
        queries = q_ref[:, h * HD : (h + 1) * HD]
        sums, accs = weigh(kb[...], queries, vt[...])
        own_sums, own_accs = weigh(k_own[...], queries, vt_own[...], seen[...])
        sum_ref[h] = sums + own_sums
        acc_ref[h] = accs + own_accs


def chunk_kernel(part_count, q_ref, acc_in, sum_in, *refs):
    parts = refs[:part_count]
    acc_ref, sum_ref, kb, vt = refs[part_count:]

    @pl.when(pl.program_id(0) == 0)
    def _():
        load_chunks(parts, kb, vt)

    for h in range(STEP_HEADS):
        sums, accs = weigh(kb[...], q_ref[:, h * HD : (h + 1) * HD], vt[...])
        sum_ref[h] = sum_in[h] + sums
        acc_ref[h] = acc_in[h] + accs


def last_kernel(part_count, slabs, *refs):
    tree_ref, len_ref, q_ref, acc_in, sum_in = refs[:5]
    parts = refs[5 : 5 + part_count]
    refs = refs[5 + part_count :]
    q_all, k_own, v_own, held = refs[0], refs[1], refs[2], refs[3 : 3 + len(slabs)]
    out_ref, kb, vt, low, high, slab, q_buf, own_buf = refs[3 + len(slabs) :]
    step = pl.program_id(0)

    @pl.when(step == 0)
    def _():
        load_chunks(parts, kb, vt)
        low[...] = jnp.full_like(low, 1.0)
        high[...] = jnp.full_like(high, 1.0)

    live = lax.broadcasted_iota(jnp.int32, (ROWS, HD), 0) < len_ref[0]
    for h in range(STEP_HEADS):
        sums, accs = weigh(kb[...], q_ref[:, h * HD : (h + 1) * HD], vt[...])
        total = jnp.sum(sum_in[h] + sums, axis=0, keepdims=True)
        low[...] = jnp.minimum(low[...], total)
        high[...] = jnp.maximum(high[...], total)
        shown = ((acc_in[h] + accs) / total).T
        cols = pl.ds(pl.multiple_of((step * STEP_HEADS + h) * HD, HD), HD)
        out_ref[:, cols] = jnp.where(live, shown, 0.0).astype(jnp.bfloat16)

    @pl.when(step == pl.num_programs(0) - 1)
    def _():
        good = (jnp.min(low[...]) > LOW) & (jnp.max(high[...]) < HIGH)

        @pl.when(jnp.logical_not(good))
        def _():
            pltpu.sync_copy(k_own, own_buf.at[0])
            pltpu.sync_copy(v_own, own_buf.at[1])

            def one_head(h, unused):
                at = pl.multiple_of(h * HD, HD)
                pltpu.sync_copy(q_all.at[:, pl.ds(at, HD)], q_buf)
                queries = q_buf[...]
                carried = fresh(ROWS)
                for ref, starts in zip(held, slabs):
                    for start in starts:
                        pltpu.sync_copy(ref.at[pl.ds(start, 16)], slab)
                        carried = online(
                            carried, token_rows(slab[:, 0]), token_rows(slab[:, 1]).T, queries, None
                        )
                visible = tree_seen(tree_ref, len_ref)
                run_max, run_sum, run_acc = online(
                    carried, own_buf[0], own_buf[1].T, queries, visible
                )
                shown = jnp.where(live, (run_acc / run_sum).T, 0.0)
                out_ref[:, pl.ds(at, HD)] = shown.astype(jnp.bfloat16)
                return unused

            lax.fori_loop(0, GROUP, one_head, 0)


def prompt_kernel(place_ref, q_ref, *refs):
    here, here_s, wide, wide_s, far, far_s, out_ref, kb, vb, vt, acc, total, top = refs
    y, z, x, core = (place_ref[i] for i in range(4))
    heads = GROUP // 2
    pair = 2 * ROWS
    for ref, core_from in ((here, core), (here_s, 1 - core)):
        for i, z_step in enumerate(STEPS):
            for j, x_step in enumerate(STEPS):
                x0, z0 = (x - x_step) % 4, (z - z_step) % 4
                at = (z0 // 2) * ROWS + ((x0 * 2 + z0 % 2) * 2 + core_from) * SUB
                spot = pl.ds(pl.multiple_of(at, SUB), SUB)
                kb[0, spot, :] = ref[i * 4 + j, 0]
                vb[spot, :] = ref[i * 4 + j, 1]
    vt[0] = vb[...].T
    others = [(wide,), (wide_s,), (far, far_s)]
    sources = [(y + 3 + 2 * core) % 4, (y + 1 + 2 * core) % 4, (y + 2) % 4]

    def queries(h):
        return q_ref[:, h * HD : (h + 1) * HD]

    key_at = lax.broadcasted_iota(jnp.int32, (pair, ROWS), 0)
    row_at = lax.broadcasted_iota(jnp.int32, (pair, ROWS), 1) + z // 2 * ROWS
    visible = key_at <= row_at
    hidden = jnp.where(visible, 0.0, -jnp.inf)
    for h in range(heads):
        total[h], acc[h] = weigh(kb[0], queries(h), vt[0], hidden)
    for i, (parts, y_from) in enumerate(zip(others, sources)):

        @pl.when(y_from < y)
        def _(i=i, parts=parts):
            load_chunks(parts, kb.at[i + 1], vt.at[i + 1])
            for h in range(heads):
                sums, accs = weigh(kb[i + 1], queries(h), vt[i + 1])
                total[h] += sums
                acc[h] += accs

    def store(h, sums):
        out_ref[:, h * HD : (h + 1) * HD] = (acc[h] / sums).T.astype(jnp.bfloat16)

    least = most = jnp.ones((1, ROWS), jnp.float32)
    for h in range(heads):
        sums = jnp.sum(total[h], axis=0, keepdims=True)
        store(h, sums)
        least, most = jnp.minimum(least, sums), jnp.maximum(most, sums)
    good = (jnp.min(least) > LOW) & (jnp.max(most) < HIGH)

    @pl.when(jnp.logical_not(good))
    def _():
        for h in range(heads):
            carried = online(fresh(ROWS), kb[0], vt[0], queries(h), visible)
            top[...], total[h, 0:1], acc[h] = carried
            for i, y_from in enumerate(sources):

                @pl.when(y_from < y)
                def _(h=h, i=i):
                    carried = (top[...], total[h, 0:1], acc[h])
                    carried = online(carried, kb[i + 1], vt[i + 1], queries(h), None)
                    top[...], total[h, 0:1], acc[h] = carried

            store(h, total[h, 0:1])


def whole(shape):
    return pl.BlockSpec(shape, lambda h: (0,) * len(shape))


STATE = (
    jax.ShapeDtypeStruct((GROUP, HD, ROWS), jnp.float32),
    jax.ShapeDtypeStruct((GROUP, 8, ROWS), jnp.float32),
)
STATE_SPECS = (
    pl.BlockSpec((STEP_HEADS, HD, ROWS), lambda h: (h, 0, 0)),
    pl.BlockSpec((STEP_HEADS, 8, ROWS), lambda h: (h, 0, 0)),
)
HEAD_SPEC = pl.BlockSpec((ROWS, STEP_HEADS * HD), lambda h: (0, h))
SCALAR = pl.BlockSpec(memory_space=pltpu.SMEM)
PARAMS = dict(compiler_params=pltpu.CompilerParams(vmem_limit_bytes=48 * MIB))


def cost(rows, keys):
    return pl.CostEstimate(
        flops=8 * rows * keys * HD, bytes_accessed=6 * MIB, transcendentals=rows * keys
    )


def attend_first(tree, length, q, k_own, v_own, parts):
    tokens = sum(part.shape[0] for part in parts) * SUB
    return pl.pallas_call(
        functools.partial(first_kernel, len(parts)),
        grid=(GROUP // STEP_HEADS,),
        in_specs=[SCALAR, SCALAR, HEAD_SPEC, whole(k_own.shape), whole(v_own.shape)]
        + [whole(part.shape) for part in parts],
        out_specs=STATE_SPECS,
        out_shape=STATE,
        scratch_shapes=[
            pltpu.VMEM((tokens, HD), jnp.bfloat16),
            pltpu.VMEM((HD, tokens), jnp.bfloat16),
            pltpu.VMEM((HD, ROWS), jnp.bfloat16),
            pltpu.VMEM((ROWS, ROWS), jnp.float32),
        ],
        cost_estimate=cost(GROUP * ROWS, tokens + ROWS),
        name="first_keys",
        **PARAMS,
    )(tree, length, q, k_own, v_own, *parts)


def attend_chunk(q, state, parts, name):
    tokens = sum(part.shape[0] for part in parts) * SUB
    return pl.pallas_call(
        functools.partial(chunk_kernel, len(parts)),
        grid=(GROUP // STEP_HEADS,),
        in_specs=[HEAD_SPEC, *STATE_SPECS] + [whole(part.shape) for part in parts],
        out_specs=STATE_SPECS,
        out_shape=STATE,
        scratch_shapes=[
            pltpu.VMEM((tokens, HD), jnp.bfloat16),
            pltpu.VMEM((HD, tokens), jnp.bfloat16),
        ],
        cost_estimate=cost(GROUP * ROWS, tokens),
        name=name,
        **PARAMS,
    )(q, *state, *parts)


def attend_last(tree, length, q, state, parts, k_own, v_own, held):
    tokens = sum(part.shape[0] for part in parts) * SUB
    slabs = tuple(tuple(range(0, part.shape[0], 16)) for part in held)
    anywhere = pl.BlockSpec(memory_space=pl.ANY)
    return pl.pallas_call(
        functools.partial(last_kernel, len(parts), slabs),
        grid=(GROUP // STEP_HEADS,),
        in_specs=[SCALAR, SCALAR, HEAD_SPEC, *STATE_SPECS]
        + [whole(part.shape) for part in parts]
        + [anywhere] * (3 + len(held)),
        out_specs=whole((ROWS, GROUP * HD)),
        out_shape=jax.ShapeDtypeStruct((ROWS, GROUP * HD), jnp.bfloat16),
        scratch_shapes=[
            pltpu.VMEM((tokens, HD), jnp.bfloat16),
            pltpu.VMEM((HD, tokens), jnp.bfloat16),
            pltpu.VMEM((1, ROWS), jnp.float32),
            pltpu.VMEM((1, ROWS), jnp.float32),
            pltpu.VMEM((16, 2, SUB, HD), jnp.bfloat16),
            pltpu.VMEM((ROWS, HD), jnp.bfloat16),
            pltpu.VMEM((2, ROWS, HD), jnp.bfloat16),
        ],
        cost_estimate=cost(GROUP * ROWS, tokens),
        name="last_keys",
        **PARAMS,
    )(tree, length, q, *state, *parts, q, k_own, v_own, *held)


def attend_prompt(place, q, parts):
    vmem = pl.BlockSpec(memory_space=pltpu.VMEM)
    heads, pair = GROUP // 2, 2 * ROWS
    return pl.pallas_call(
        prompt_kernel,
        in_specs=[SCALAR] + [vmem] * (1 + len(parts)),
        out_specs=vmem,
        out_shape=jax.ShapeDtypeStruct(q.shape, jnp.bfloat16),
        scratch_shapes=[
            pltpu.VMEM((4, pair, HD), jnp.bfloat16),
            pltpu.VMEM((pair, HD), jnp.bfloat16),
            pltpu.VMEM((4, HD, pair), jnp.bfloat16),
            pltpu.VMEM((heads, HD, ROWS), jnp.float32),
            pltpu.VMEM((heads, 8, ROWS), jnp.float32),
            pltpu.VMEM((1, ROWS), jnp.float32),
        ],
        cost_estimate=cost(heads * ROWS, 4 * pair),
        name="prompt_rows",
        **PARAMS,
    )(place, q, *parts)


def after(value, *events):
    return lax.optimization_barrier((value, *events))[0]


def on_device(q_prompt, k_prompt, v_prompt, q_resp, k_resp, v_resp, tree_table, lengths):
    chain, resp = lax.axis_index("chain"), lax.axis_index("resp")
    y, z, x, core = chain // 2, chain % 2 * 2 + resp // 2 % 2, resp // 4, resp % 2
    place = jnp.stack([y, z, x, core]).astype(jnp.int32)
    q = q_resp[0]

    def cols(block, at, count):
        return lax.dynamic_slice_in_dim(block, at * count * HD, count * HD, block.ndim - 1)

    tokens = jnp.stack([k_prompt, v_prompt])
    over_y, over_x = [cols(tokens, y, 2)], [cols(tokens, x, 2)]
    for d in STEPS[1:]:
        over_y.append(move(cols(tokens, (y + d) % 4, 2), along_y(d)))
        over_x.append(move(cols(tokens, (x + d) % 4, 2), along_x(d)))
    over_y, over_x = jnp.stack(over_y), jnp.stack(over_x)

    def for_z(at):
        return jnp.stack([cols(over_y, at // 2, 1), cols(over_x, at % 2, 1)])

    over_z = [for_z(z)] + [move(for_z((z + d) % 4), along_z(d)) for d in STEPS[1:]]
    here = jnp.concatenate(over_z, 1)
    here_s = move(here, other_core)
    r_here, p_here, r_here_s, p_here_s = here[0], here[1], here_s[0], here_s[1]
    r_wide = move(jnp.concatenate([r_here, r_here_s]), both_ways_x)
    p_wide = move(jnp.concatenate([p_here, p_here_s]), both_ways_y)

    state = attend_first(tree_table, lengths, q, k_resp[0], v_resp[0], (r_here, r_here_s))
    r_wide, p_wide = after((r_wide, p_wide), state[1])
    r_far, p_far = move(r_wide[:16], both_ways_x), move(p_wide[:16], both_ways_y)
    r_wide_s, p_wide_s = move(r_wide, other_core), move(p_wide, other_core)
    state = attend_chunk(q, state, (r_wide,), "wide_keys")
    r_far, p_far = after((r_far, p_far), state[1])
    r_far_s, p_far_s = move(r_far, other_core), move(p_far, other_core)
    state = attend_chunk(q, state, (r_wide_s,), "wide_keys_s")
    prompt_out = attend_prompt(
        place, q_prompt, (p_here, p_here_s, p_wide, p_wide_s, p_far, p_far_s)
    )
    held = (r_here, r_here_s, r_wide, r_wide_s, r_far, r_far_s)
    resp_out = attend_last(
        tree_table, lengths, q, state, (r_far, r_far_s), k_resp[0], v_resp[0], held
    )
    return (prompt_out, resp_out[None])


def solution(mesh):
    placed = (
        P("chain", "resp"),
        P(("chain", "resp"), None),
        P(("chain", "resp"), None),
        P("resp", None, "chain"),
        P("resp", None, "chain"),
        P("resp", None, "chain"),
        P("resp", None),
        P("resp"),
    )
    return jax.shard_map(
        on_device,
        mesh=mesh,
        in_specs=placed,
        out_specs=(P("chain", "resp"), P("resp", None, "chain")),
        check_vma=False,
    )
```

```python
import functools

import jax
import jax.numpy as jnp
from jax import lax
from jax.experimental import pallas as pl
from jax.experimental.pallas import tpu as pltpu
from jax.sharding import PartitionSpec as P

QH = 64
KVH = 8
HD = 128
RBLK = 8
ROWS = 512
SUB = 32
GROUP = QH // KVH
STEP_HEADS = 4
SCALE = HD**-0.5 * 1.4426950408889634
LOW, HIGH = 1e-18, 1e30
AXES = ("chain", "resp")
STEPS = (0, 1, 3, 2)
CHUNKS = 4
MIB = 2**20
PLACES = [(y, z, x, k) for y in range(4) for z in range(4) for x in range(4) for k in range(2)]


def device_at(y, z, x, core):
    return (y * 2 + z // 2) * 16 + (x * 2 + z % 2) * 2 + core


def move(block, target):
    route = [(device_at(*p), device_at(*target(*p))) for p in PLACES]
    return lax.ppermute(block, AXES, route)


def first_axis(d):
    def target(y, z, x, core):
        return (y, z, (x + d) % 4, core) if core else ((y + d) % 4, z, x, core)

    return target


def along_z(d):
    return lambda y, z, x, core: (y, (z + d) % 4, x, core)


def last_axis(d):
    def target(y, z, x, core):
        return ((y + d) % 4, z, x, core) if core else (y, z, (x + d) % 4, core)

    return target


def other_core(y, z, x, core):
    return (y, z, x, 1 - core)


def dot_t(a, b):
    return lax.dot_general(a, b, (((1,), (1,)), ((), ())), preferred_element_type=jnp.float32)


def fold_rows(p):
    return jnp.sum(p.reshape(p.shape[0] // 8, 8, p.shape[1]), axis=0)


def token_rows(block):
    return block.reshape(-1, HD)


def online(carried, keys, values_t, queries, visible):
    run_max, run_sum, run_acc = carried
    scores = dot_t(keys, queries) * SCALE
    if visible is not None:
        scores = jnp.where(visible, scores, -1e30)
    new_max = jnp.maximum(run_max, jnp.max(scores, axis=0, keepdims=True))
    weights = jnp.exp2(scores - new_max)
    if visible is not None:
        weights = jnp.where(visible, weights, 0.0)
    rescale = jnp.exp2(run_max - new_max)
    run_sum = run_sum * rescale + jnp.sum(weights, axis=0, keepdims=True)
    added = jnp.dot(values_t, weights.astype(jnp.bfloat16), preferred_element_type=jnp.float32)
    return (new_max, run_sum, run_acc * rescale + added)


def fresh(cols):
    return (
        jnp.full((1, cols), -1e30, jnp.float32),
        jnp.zeros((1, cols), jnp.float32),
        jnp.zeros((HD, cols), jnp.float32),
    )


def tree_seen(tree_ref, len_ref):
    lines = []
    for j in range(RBLK):
        parent = tree_ref[0, j]
        line = jnp.int32(1 << j)
        for i in range(j):
            line = line | jnp.where(parent == i, lines[i], 0)
        lines.append(line)
    key_at = lax.broadcasted_iota(jnp.int32, (ROWS, ROWS), 0)
    row_at = lax.broadcasted_iota(jnp.int32, (ROWS, ROWS), 1)
    span = ROWS // RBLK
    line_of_row = jnp.zeros((ROWS, ROWS), jnp.int32)
    for j in range(RBLK):
        line_of_row = jnp.where(row_at // span == j, lines[j], line_of_row)
    related = (lax.shift_right_logical(line_of_row, key_at // span) & 1) == 1
    return related & (key_at <= row_at) & (key_at < len_ref[0])


def own_kernel(tree_ref, len_ref, q_ref, k_ref, v_ref, acc_ref, sum_ref, vt, seen):
    @pl.when(pl.program_id(0) == 0)
    def _():
        vt[...] = v_ref[...].T
        seen[...] = jnp.where(tree_seen(tree_ref, len_ref), 0.0, -jnp.inf)

    for h in range(STEP_HEADS):
        queries = q_ref[:, h * HD : (h + 1) * HD]
        sum_ref[h], acc_ref[h] = weigh(k_ref[...], queries, vt[...], seen[...])


def load_tokens(part, kb, vt):
    kb[...] = token_rows(part[:, 0])
    vt[...] = token_rows(part[:, 1]).T


def load_chunk(from_here, here, other, kb, vt):
    @pl.when(from_here)
    def _():
        load_tokens(here, kb, vt)

    @pl.when(jnp.logical_not(from_here))
    def _():
        load_tokens(other, kb, vt)


def weigh(keys, queries, values_t, shown=None):
    scores = dot_t(keys, queries) * SCALE
    weights = jnp.exp2(scores if shown is None else scores + shown)
    added = jnp.dot(values_t, weights.astype(jnp.bfloat16), preferred_element_type=jnp.float32)
    return fold_rows(weights), added


def chunk_kernel(place_ref, q_ref, acc_in, sum_in, here, other, acc_ref, sum_ref, kb, vt):
    @pl.when(pl.program_id(0) == 0)
    def _():
        load_chunk(place_ref[3] == 0, here, other, kb, vt)

    for h in range(STEP_HEADS):
        sums, accs = weigh(kb[...], q_ref[:, h * HD : (h + 1) * HD], vt[...])
        sum_ref[h] = sum_in[h] + sums
        acc_ref[h] = acc_in[h] + accs


def last_kernel(place_ref, tree_ref, len_ref, q_ref, acc_in, sum_in, here, other, *refs):
    q_all, k_own, v_own = refs[:3]
    held = refs[3 : 3 + 2 * CHUNKS]
    out_ref, kb, vt, low, high, slab, q_buf, own_buf = refs[3 + 2 * CHUNKS :]
    step = pl.program_id(0)
    is_first = place_ref[3] == 0

    @pl.when(step == 0)
    def _():
        load_chunk(is_first, here, other, kb, vt)
        low[...] = jnp.full_like(low, 1.0)
        high[...] = jnp.full_like(high, 1.0)

    live = lax.broadcasted_iota(jnp.int32, (ROWS, HD), 0) < len_ref[0]
    for h in range(STEP_HEADS):
        sums, accs = weigh(kb[...], q_ref[:, h * HD : (h + 1) * HD], vt[...])
        total = jnp.sum(sum_in[h] + sums, axis=0, keepdims=True)
        low[...] = jnp.minimum(low[...], total)
        high[...] = jnp.maximum(high[...], total)
        shown = ((acc_in[h] + accs) / total).T
        cols = pl.ds(pl.multiple_of((step * STEP_HEADS + h) * HD, HD), HD)
        out_ref[:, cols] = jnp.where(live, shown, 0.0).astype(jnp.bfloat16)

    @pl.when(step == pl.num_programs(0) - 1)
    def _():
        good = (jnp.min(low[...]) > LOW) & (jnp.max(high[...]) < HIGH)

        @pl.when(jnp.logical_not(good))
        def _():
            pltpu.sync_copy(k_own, own_buf.at[0])
            pltpu.sync_copy(v_own, own_buf.at[1])

            def one_head(h, unused):
                at = pl.multiple_of(h * HD, HD)
                pltpu.sync_copy(q_all.at[:, pl.ds(at, HD)], q_buf)
                queries = q_buf[...]
                carried = fresh(ROWS)
                for one, two in zip(held[:CHUNKS], held[CHUNKS:]):
                    for part in (pl.ds(0, 8), pl.ds(8, 8)):

                        @pl.when(is_first)
                        def _(one=one, part=part):
                            pltpu.sync_copy(one.at[part], slab)

                        @pl.when(jnp.logical_not(is_first))
                        def _(two=two, part=part):
                            pltpu.sync_copy(two.at[part], slab)

                        carried = online(
                            carried, token_rows(slab[:, 0]), token_rows(slab[:, 1]).T, queries, None
                        )
                visible = tree_seen(tree_ref, len_ref)
                run_max, run_sum, run_acc = online(
                    carried, own_buf[0], own_buf[1].T, queries, visible
                )
                shown = jnp.where(live, (run_acc / run_sum).T, 0.0)
                out_ref[:, pl.ds(at, HD)] = shown.astype(jnp.bfloat16)
                return unused

            lax.fori_loop(0, GROUP, one_head, 0)


def prompt_kernel(place_ref, q_ref, *refs):
    held = refs[: 2 * CHUNKS]
    out_ref, kb, vb, vt, acc, total, top = refs[2 * CHUNKS :]
    y, z, x, core = (place_ref[i] for i in range(4))
    heads = GROUP // 2
    pair = 2 * ROWS
    is_second = core == 1

    def load_own(ref):
        for i, z_step in enumerate(STEPS):
            for j, x_step in enumerate(STEPS):
                x0, z0 = (x - x_step) % 4, (z - z_step) % 4
                for lane in range(2):
                    at = (z0 // 2) * ROWS + ((x0 * 2 + z0 % 2) * 2 + 1 - lane) * SUB
                    spot = pl.ds(pl.multiple_of(at, SUB), SUB)
                    kb[0, spot, :] = ref[i * 4 + j, 0, lane * SUB : (lane + 1) * SUB]
                    vb[spot, :] = ref[i * 4 + j, 1, lane * SUB : (lane + 1) * SUB]

    @pl.when(is_second)
    def _():
        load_own(held[0])

    @pl.when(jnp.logical_not(is_second))
    def _():
        load_own(held[CHUNKS])

    vt[0] = vb[...].T
    sources = [(y + 3) % 4, (y + 1) % 4, (y + 2) % 4]

    def queries(h):
        return q_ref[:, h * HD : (h + 1) * HD]

    key_at = lax.broadcasted_iota(jnp.int32, (pair, ROWS), 0)
    row_at = lax.broadcasted_iota(jnp.int32, (pair, ROWS), 1) + z // 2 * ROWS
    visible = key_at <= row_at
    hidden = jnp.where(visible, 0.0, -jnp.inf)
    for h in range(heads):
        total[h], acc[h] = weigh(kb[0], queries(h), vt[0], hidden)
    for i, y_from in enumerate(sources, 1):

        @pl.when(y_from < y)
        def _(i=i):
            load_chunk(is_second, held[i], held[CHUNKS + i], kb.at[i], vt.at[i])
            for h in range(heads):
                sums, accs = weigh(kb[i], queries(h), vt[i])
                total[h] += sums
                acc[h] += accs

    def store(h, sums):
        out_ref[:, h * HD : (h + 1) * HD] = (acc[h] / sums).T.astype(jnp.bfloat16)

    least = most = jnp.ones((1, ROWS), jnp.float32)
    for h in range(heads):
        sums = jnp.sum(total[h], axis=0, keepdims=True)
        store(h, sums)
        least, most = jnp.minimum(least, sums), jnp.maximum(most, sums)
    good = (jnp.min(least) > LOW) & (jnp.max(most) < HIGH)

    @pl.when(jnp.logical_not(good))
    def _():
        for h in range(heads):
            carried = online(fresh(ROWS), kb[0], vt[0], queries(h), visible)
            top[...], total[h, 0:1], acc[h] = carried
            for i, y_from in enumerate(sources, 1):

                @pl.when(y_from < y)
                def _(h=h, i=i):
                    carried = (top[...], total[h, 0:1], acc[h])
                    carried = online(carried, kb[i], vt[i], queries(h), None)
                    top[...], total[h, 0:1], acc[h] = carried

            store(h, total[h, 0:1])


def whole(shape):
    return pl.BlockSpec(shape, lambda h: (0,) * len(shape))


STATE = (
    jax.ShapeDtypeStruct((GROUP, HD, ROWS), jnp.float32),
    jax.ShapeDtypeStruct((GROUP, 8, ROWS), jnp.float32),
)
STATE_SPECS = (
    pl.BlockSpec((STEP_HEADS, HD, ROWS), lambda h: (h, 0, 0)),
    pl.BlockSpec((STEP_HEADS, 8, ROWS), lambda h: (h, 0, 0)),
)
HEAD_SPEC = pl.BlockSpec((ROWS, STEP_HEADS * HD), lambda h: (0, h))
SCALAR = pl.BlockSpec(memory_space=pltpu.SMEM)
PARAMS = dict(compiler_params=pltpu.CompilerParams(vmem_limit_bytes=32 * MIB))


def cost(rows, keys):
    return pl.CostEstimate(
        flops=8 * rows * keys * HD, bytes_accessed=6 * MIB, transcendentals=rows * keys
    )


def attend_own(tree, length, q, k, v):
    return pl.pallas_call(
        own_kernel,
        grid=(GROUP // STEP_HEADS,),
        in_specs=[SCALAR, SCALAR, HEAD_SPEC, whole(k.shape), whole(v.shape)],
        out_specs=STATE_SPECS,
        out_shape=STATE,
        scratch_shapes=[
            pltpu.VMEM((HD, ROWS), jnp.bfloat16),
            pltpu.VMEM((ROWS, ROWS), jnp.float32),
        ],
        cost_estimate=cost(GROUP * ROWS, ROWS),
        name="own_keys",
        **PARAMS,
    )(tree, length, q, k, v)


def chunk_scratch():
    return [
        pltpu.VMEM((2 * ROWS, HD), jnp.bfloat16),
        pltpu.VMEM((HD, 2 * ROWS), jnp.bfloat16),
    ]


def attend_chunk(place, q, state, here, other, name):
    return pl.pallas_call(
        chunk_kernel,
        grid=(GROUP // STEP_HEADS,),
        in_specs=[SCALAR, HEAD_SPEC, *STATE_SPECS, whole(here.shape), whole(other.shape)],
        out_specs=STATE_SPECS,
        out_shape=STATE,
        scratch_shapes=chunk_scratch(),
        cost_estimate=cost(GROUP * ROWS, 2 * ROWS),
        name=name,
        **PARAMS,
    )(place, q, *state, here, other)


def attend_last(place, tree, length, q, state, here, other, k_own, v_own, held):
    anywhere = pl.BlockSpec(memory_space=pl.ANY)
    return pl.pallas_call(
        last_kernel,
        grid=(GROUP // STEP_HEADS,),
        in_specs=[SCALAR, SCALAR, SCALAR, HEAD_SPEC, *STATE_SPECS]
        + [whole(here.shape), whole(other.shape)]
        + [anywhere] * (3 + len(held)),
        out_specs=whole((ROWS, GROUP * HD)),
        out_shape=jax.ShapeDtypeStruct((ROWS, GROUP * HD), jnp.bfloat16),
        scratch_shapes=chunk_scratch()
        + [
            pltpu.VMEM((1, ROWS), jnp.float32),
            pltpu.VMEM((1, ROWS), jnp.float32),
            pltpu.VMEM((8, 2, 2 * SUB, HD), jnp.bfloat16),
            pltpu.VMEM((ROWS, HD), jnp.bfloat16),
            pltpu.VMEM((2, ROWS, HD), jnp.bfloat16),
        ],
        cost_estimate=cost(GROUP * ROWS, 2 * ROWS),
        name="last_keys",
        **PARAMS,
    )(place, tree, length, q, *state, here, other, q, k_own, v_own, *held)


def attend_prompt(place, q, held):
    vmem = pl.BlockSpec(memory_space=pltpu.VMEM)
    heads, pair = GROUP // 2, 2 * ROWS
    return pl.pallas_call(
        prompt_kernel,
        in_specs=[SCALAR] + [vmem] * (1 + len(held)),
        out_specs=vmem,
        out_shape=jax.ShapeDtypeStruct(q.shape, jnp.bfloat16),
        scratch_shapes=[
            pltpu.VMEM((4, pair, HD), jnp.bfloat16),
            pltpu.VMEM((pair, HD), jnp.bfloat16),
            pltpu.VMEM((4, HD, pair), jnp.bfloat16),
            pltpu.VMEM((heads, HD, ROWS), jnp.float32),
            pltpu.VMEM((heads, 8, ROWS), jnp.float32),
            pltpu.VMEM((1, ROWS), jnp.float32),
        ],
        cost_estimate=cost(heads * ROWS, 4 * pair),
        name="prompt_rows",
        **PARAMS,
    )(place, q, *held)


def after(value, *events):
    return lax.optimization_barrier((value, *events))[0]


def on_device(q_prompt, k_prompt, v_prompt, q_resp, k_resp, v_resp, tree_table, lengths):
    chain, resp = lax.axis_index("chain"), lax.axis_index("resp")
    y, z, x, core = chain // 2, chain % 2 * 2 + resp // 2 % 2, resp // 4, resp % 2
    place = jnp.stack([y, z, x, core]).astype(jnp.int32)
    q = q_resp[0]

    def cols(block, at, count):
        return lax.dynamic_slice_in_dim(block, at * count * HD, count * HD, block.ndim - 1)

    tokens = jnp.stack([k_prompt, v_prompt])
    tokens = jnp.concatenate([tokens, move(tokens, other_core)], 1)
    near = jnp.where(core == 0, y, x)
    over = [cols(tokens, near, 2)]
    over += [move(cols(tokens, (near + d) % 4, 2), first_axis(d)) for d in STEPS[1:]]
    over = jnp.stack(over)

    def for_z(at):
        return cols(over, jnp.where(core == 0, at // 2, at % 2), 1)

    over_z = [for_z(z)] + [move(for_z((z + d) % 4), along_z(d)) for d in STEPS[1:]]
    state = attend_own(tree_table, lengths, after(q, over), k_resp[0], v_resp[0])
    over_z = after(over_z, state[1])
    here = jnp.concatenate(over_z)
    here_o = move(here, other_core)
    left, right = move(here, last_axis(1)), move(here, last_axis(3))
    state = attend_chunk(place, q, state, here, here_o, "here_keys")
    left, right = after((left, right), state[1])
    left_o, right_o = move(left, other_core), move(right, other_core)
    far_l, far_r = move(left[:8], last_axis(1)), move(right[8:], last_axis(3))
    state = attend_chunk(place, q, state, left, left_o, "left_keys")
    far_l, far_r = after((far_l, far_r), state[1])
    far = jnp.concatenate([far_l, far_r])
    far_o = move(far, other_core)
    state = attend_chunk(place, q, state, right, right_o, "right_keys")
    held = (here, left, right, far, here_o, left_o, right_o, far_o)
    prompt_out = attend_prompt(place, q_prompt, held)
    resp_out = attend_last(
        place, tree_table, lengths, q, state, far, far_o, k_resp[0], v_resp[0], held
    )
    return (prompt_out, resp_out[None])


def solution(mesh):
    placed = (
        P("chain", "resp"),
        P(("chain", "resp"), None),
        P(("chain", "resp"), None),
        P("resp", None, "chain"),
        P("resp", None, "chain"),
        P("resp", None, "chain"),
        P("resp", None),
        P("resp"),
    )
    return jax.shard_map(
        on_device,
        mesh=mesh,
        in_specs=placed,
        out_specs=(P("chain", "resp"), P("resp", None, "chain")),
        check_vma=False,
    )
```

```python
import functools

import jax
import jax.numpy as jnp
from jax import lax
from jax.experimental import pallas as pl
from jax.experimental.pallas import tpu as pltpu
from jax.sharding import PartitionSpec as P

QH = 64
KVH = 8
HD = 128
RBLK = 8
ROWS = 512
SUB = 32
GROUP = QH // KVH
STEP_HEADS = 4
SCALE = HD**-0.5 * 1.4426950408889634
LOW, HIGH = 1e-18, 1e30
AXES = ("chain", "resp")
STEPS = (0, 1, 3, 2)
CHUNKS = 4
MIB = 2**20
PLACES = [(y, z, x, k) for y in range(4) for z in range(4) for x in range(4) for k in range(2)]


def device_at(y, z, x, core):
    return (y * 2 + z // 2) * 16 + (x * 2 + z % 2) * 2 + core


def move(block, target):
    route = [(device_at(*p), device_at(*target(*p))) for p in PLACES]
    return lax.ppermute(block, AXES, route)


def first_axis(d):
    def target(y, z, x, core):
        return (y, z, (x + d) % 4, core) if core else ((y + d) % 4, z, x, core)

    return target


def along_z(d):
    return lambda y, z, x, core: (y, (z + d) % 4, x, core)


def last_axis(d):
    def target(y, z, x, core):
        return ((y + d) % 4, z, x, core) if core else (y, z, (x + d) % 4, core)

    return target


def other_core(y, z, x, core):
    return (y, z, x, 1 - core)


def dot_t(a, b):
    return lax.dot_general(a, b, (((1,), (1,)), ((), ())), preferred_element_type=jnp.float32)


def fold_rows(p):
    return jnp.sum(p.reshape(p.shape[0] // 8, 8, p.shape[1]), axis=0)


def online(carried, keys, values_t, queries, visible):
    run_max, run_sum, run_acc = carried
    scores = dot_t(keys, queries) * SCALE
    if visible is not None:
        scores = jnp.where(visible, scores, -1e30)
    new_max = jnp.maximum(run_max, jnp.max(scores, axis=0, keepdims=True))
    weights = jnp.exp2(scores - new_max)
    if visible is not None:
        weights = jnp.where(visible, weights, 0.0)
    rescale = jnp.exp2(run_max - new_max)
    run_sum = run_sum * rescale + jnp.sum(weights, axis=0, keepdims=True)
    added = jnp.dot(values_t, weights.astype(jnp.bfloat16), preferred_element_type=jnp.float32)
    return (new_max, run_sum, run_acc * rescale + added)


def fresh(cols):
    return (
        jnp.full((1, cols), -1e30, jnp.float32),
        jnp.zeros((1, cols), jnp.float32),
        jnp.zeros((HD, cols), jnp.float32),
    )


def tree_seen(tree_ref, len_ref):
    lines = []
    for j in range(RBLK):
        parent = tree_ref[0, j]
        line = jnp.int32(1 << j)
        for i in range(j):
            line = line | jnp.where(parent == i, lines[i], 0)
        lines.append(line)
    key_at = lax.broadcasted_iota(jnp.int32, (ROWS, ROWS), 0)
    row_at = lax.broadcasted_iota(jnp.int32, (ROWS, ROWS), 1)
    span = ROWS // RBLK
    line_of_row = jnp.zeros((ROWS, ROWS), jnp.int32)
    for j in range(RBLK):
        line_of_row = jnp.where(row_at // span == j, lines[j], line_of_row)
    related = (lax.shift_right_logical(line_of_row, key_at // span) & 1) == 1
    return related & (key_at <= row_at) & (key_at < len_ref[0])


def weigh(keys, queries, values_t, shown=None):
    scores = dot_t(keys, queries) * SCALE
    weights = jnp.exp2(scores if shown is None else scores + shown)
    added = jnp.dot(values_t, weights.astype(jnp.bfloat16), preferred_element_type=jnp.float32)
    return fold_rows(weights), added


def over_heads(one_head):
    def some(step, unused):
        for h in range(STEP_HEADS):
            head = step * STEP_HEADS + h
            one_head(head, pl.ds(pl.multiple_of(head * HD, HD), HD))
        return unused

    lax.fori_loop(0, GROUP // STEP_HEADS, some, 0)


def own_kernel(tree_ref, len_ref, q_ref, k_ref, v_ref, acc_ref, sum_ref, vt, seen):
    vt[...] = v_ref[...].T
    seen[...] = jnp.where(tree_seen(tree_ref, len_ref), 0.0, -jnp.inf)

    def one_head(h, cols):
        sum_ref[h], acc_ref[h] = weigh(k_ref[...], q_ref[:, cols], vt[...], seen[...])

    over_heads(one_head)


def pick_kernel(place_ref, own, k_other, v_other, *outs):
    near = jnp.where(place_ref[3] == 0, place_ref[0], place_ref[2])
    for step, out_ref in zip(STEPS, outs):
        width = 2 * HD
        cols = pl.ds(pl.multiple_of((near + step) % 4 * width, width), width)
        for i, other in enumerate((k_other, v_other)):
            out_ref[i, :SUB, :] = own[i, :, cols]
            out_ref[i, SUB:, :] = other[:, cols]


def arrange_kernel(*refs):
    out_ref = refs[4]
    for i, ref in enumerate(refs[:4]):
        for half in range(2):
            pieces = ref[2 * half : 2 * half + 2]
            out_ref[2 * i + half, 0] = pieces[:, 0].reshape(HD, HD)
            out_ref[2 * i + half, 1] = pieces[:, 1].reshape(HD, HD).T


def load_blocks(chunk, kb, vt):
    for b in range(8):
        kb[b * HD : (b + 1) * HD, :] = chunk[b, 0]
        vt[:, b * HD : (b + 1) * HD] = chunk[b, 1]


def load_chunk(from_here, here, other, kb, vt):
    @pl.when(from_here)
    def _():
        load_blocks(here, kb, vt)

    @pl.when(jnp.logical_not(from_here))
    def _():
        load_blocks(other, kb, vt)


def chunk_kernel(place_ref, q_ref, acc_in, sum_in, here, other, acc_ref, sum_ref, kb, vt):
    load_chunk(place_ref[3] == 0, here, other, kb, vt)

    def one_head(h, cols):
        sums, accs = weigh(kb[...], q_ref[:, cols], vt[...])
        sum_ref[h] = sum_in[h] + sums
        acc_ref[h] = acc_in[h] + accs

    over_heads(one_head)


def in_range(low, high):
    return (jnp.min(low) > LOW) & (jnp.max(high) < HIGH)


def prompt_part(place_ref, q_ref, acc_in, sum_in, held, out_ref, kb, vt, seen, acc, total, top):
    is_second = place_ref[3] == 1
    acc[...] = acc_in[...]
    total[...] = sum_in[...]

    def queries(h):
        return q_ref[:, h * HD : (h + 1) * HD]

    def earlier_pairs(body):
        def one_pair(i, unused):
            for at, spot in enumerate((1, 3, 2)):

                @pl.when(i == at)
                def _(spot=spot):
                    load_chunk(is_second, held[spot], held[CHUNKS + spot], kb, vt)

            body()
            return unused

        lax.fori_loop(0, place_ref[0], one_pair, 0)

    def add():
        for h in range(HALF_HEADS):
            sums, accs = weigh(kb[...], queries(h), vt[...])
            total[h] += sums
            acc[h] += accs

    earlier_pairs(add)

    def store(h, sums):
        shown = (acc[h] * (1.0 / sums)).astype(jnp.bfloat16)
        out_ref[:, h * HD : (h + 1) * HD] = shown.T

    low = high = jnp.ones((1, ROWS), jnp.float32)
    for h in range(HALF_HEADS):
        sums = jnp.sum(total[h], axis=0, keepdims=True)
        store(h, sums)
        low, high = jnp.minimum(low, sums), jnp.maximum(high, sums)

    @pl.when(jnp.logical_not(in_range(low, high)))
    def _():
        load_chunk(is_second, held[0], held[CHUNKS], kb, vt)
        for rows, visible in own_pair_seen(place_ref):
            seen[rows, :] = jnp.where(visible, 1.0, 0.0)
        top[...] = jnp.full_like(top, -1e30)
        total[...] = jnp.zeros_like(total)
        acc[...] = jnp.zeros_like(acc)

        def exact():
            def one_head(h, unused):
                cols = pl.ds(pl.multiple_of(h * HD, HD), HD)
                carried = (top[h], total[h, 0:1], acc[h])
                carried = online(carried, kb[...], vt[...], q_ref[:, cols], seen[...] > 0.5)
                top[h], total[h, 0:1], acc[h] = carried
                return unused

            lax.fori_loop(0, HALF_HEADS, one_head, 0)

        exact()
        seen[...] = jnp.ones_like(seen)
        earlier_pairs(exact)
        for h in range(HALF_HEADS):
            store(h, total[h, 0:1])


def last_kernel(place_ref, tree_ref, len_ref, q_ref, acc_in, sum_in, *refs):
    q_rows, acc_rows, sum_rows = refs[:3]
    rows_held, (k_own, v_own), refs = refs[3 : 3 + 2 * CHUNKS], refs[11:13], refs[13:]
    held, refs = refs[: 2 * CHUNKS], refs[2 * CHUNKS :]
    out_ref, out_rows, kb, vt, low, high, block, own = refs[:8]
    prompt_part(place_ref, q_rows, acc_rows, sum_rows, rows_held, out_rows, *refs[8:])
    here, other = rows_held[CHUNKS - 1], rows_held[2 * CHUNKS - 1]
    is_first = place_ref[3] == 0
    load_chunk(is_first, here, other, kb, vt)
    low[...] = jnp.full_like(low, 1.0)
    high[...] = jnp.full_like(high, 1.0)
    live = lax.broadcasted_iota(jnp.int32, (HD, ROWS), 1) < len_ref[0]

    def store(cols, acc, total):
        shown = jnp.where(live, acc * (1.0 / total), 0.0)
        out_ref[:, cols] = shown.astype(jnp.bfloat16).T

    def one_head(h, cols):
        sums, accs = weigh(kb[...], q_ref[:, cols], vt[...])
        total = jnp.sum(sum_in[h] + sums, axis=0, keepdims=True)
        low[...] = jnp.minimum(low[...], total)
        high[...] = jnp.maximum(high[...], total)
        store(cols, acc_in[h] + accs, total)

    over_heads(one_head)

    @pl.when(jnp.logical_not(in_range(low[...], high[...])))
    def _():
        pltpu.sync_copy(k_own, own.at[0])
        pltpu.sync_copy(v_own, own.at[1])

        def exact_head(h, unused):
            cols = pl.ds(pl.multiple_of(h * HD, HD), HD)
            queries = q_ref[:, cols]

            def one_block(i, carried, one, two):
                @pl.when(is_first)
                def _():
                    pltpu.sync_copy(one.at[i], block)

                @pl.when(jnp.logical_not(is_first))
                def _():
                    pltpu.sync_copy(two.at[i], block)

                return online(carried, block[0], block[1], queries, None)

            carried = fresh(ROWS)
            for one, two in zip(held[:CHUNKS], held[CHUNKS:]):
                carried = lax.fori_loop(
                    0, 8, functools.partial(one_block, one=one, two=two), carried
                )
            visible = tree_seen(tree_ref, len_ref)
            run_max, run_sum, run_acc = online(carried, own[0], own[1].T, queries, visible)
            store(cols, run_acc, run_sum)
            return unused

        lax.fori_loop(0, GROUP, exact_head, 0)


def own_pair_seen(place_ref):
    y, z, x, core = (place_ref[i] for i in range(4))
    row_at = lax.broadcasted_iota(jnp.int32, (SUB, ROWS), 1) + z // 2 * ROWS
    key_at = lax.broadcasted_iota(jnp.int32, (SUB, ROWS), 0)
    for i, z_step in enumerate(STEPS):
        for j, x_step in enumerate(STEPS):
            x0, z0 = (x - x_step) % 4, (z - z_step) % 4
            for lane in range(2):
                first = (z0 // 2) * ROWS + ((x0 * 2 + z0 % 2) * 2 + 1 - lane) * SUB
                at = ((i * 4 + j) * 2 + lane) * SUB
                yield slice(at, at + SUB), key_at + first <= row_at


def here_kernel(place_ref, q_ref, q_rows, acc_in, sum_in, here, other, *refs):
    acc_ref, sum_ref, acc_rows, sum_rows, kb, vt, kb_rows, vt_rows, seen = refs
    chunk_kernel(place_ref, q_ref, acc_in, sum_in, here, other, acc_ref, sum_ref, kb, vt)
    load_chunk(place_ref[3] == 1, here, other, kb_rows, vt_rows)
    for rows, visible in own_pair_seen(place_ref):
        seen[rows, :] = jnp.where(visible, 0.0, -jnp.inf)
    for h in range(HALF_HEADS):
        queries = q_rows[:, h * HD : (h + 1) * HD]
        sum_rows[h], acc_rows[h] = weigh(kb_rows[...], queries, vt_rows[...], seen[...])


HALF_HEADS = GROUP // 2
PAIR = 2 * ROWS
CHUNK = jax.ShapeDtypeStruct((8, 2, HD, HD), jnp.bfloat16)


def state_of(heads):
    return (
        jax.ShapeDtypeStruct((heads, HD, ROWS), jnp.float32),
        jax.ShapeDtypeStruct((heads, 8, ROWS), jnp.float32),
    )


SCALAR = pl.BlockSpec(memory_space=pltpu.SMEM)
VMEM = pl.BlockSpec(memory_space=pltpu.VMEM)
ANYWHERE = pl.BlockSpec(memory_space=pl.ANY)
KEYS = [pltpu.VMEM((PAIR, HD), jnp.bfloat16), pltpu.VMEM((HD, PAIR), jnp.bfloat16)]


def call(kernel, name, in_specs, out_shape, scratch, rows, keys):
    single = not isinstance(out_shape, tuple)
    return pl.pallas_call(
        kernel,
        in_specs=in_specs,
        out_specs=VMEM if single else tuple(VMEM for _ in out_shape),
        out_shape=out_shape,
        scratch_shapes=scratch,
        cost_estimate=pl.CostEstimate(
            flops=8 * rows * keys * HD, bytes_accessed=6 * MIB, transcendentals=rows * keys
        ),
        compiler_params=pltpu.CompilerParams(vmem_limit_bytes=32 * MIB),
        name=name,
    )


def attend_own(tree, length, q, k, v):
    scratch = [pltpu.VMEM((HD, ROWS), jnp.bfloat16), pltpu.VMEM((ROWS, ROWS), jnp.float32)]
    specs = [SCALAR, SCALAR, VMEM, VMEM, VMEM]
    return call(own_kernel, "own_keys", specs, state_of(GROUP), scratch, GROUP * ROWS, ROWS)(
        tree, length, q, k, v
    )


def pick(place, own, k_other, v_other):
    out = tuple(jax.ShapeDtypeStruct((2, 2 * SUB, 2 * HD), jnp.bfloat16) for _ in STEPS)
    return call(pick_kernel, "pick", [SCALAR] + [VMEM] * 3, out, [], 8, 8)(
        place, own, k_other, v_other
    )


def arrange(parts):
    return call(arrange_kernel, "arrange", [VMEM] * 4, CHUNK, [], 8, 8)(*parts)


def attend_chunk(place, q, state, here, other, name):
    specs = [SCALAR] + [VMEM] * 5
    return call(chunk_kernel, name, specs, state_of(GROUP), KEYS, GROUP * ROWS, PAIR)(
        place, q, *state, here, other
    )


def attend_here(place, q, q_rows, state, here, other):
    scratch = KEYS + KEYS + [pltpu.VMEM((PAIR, ROWS), jnp.float32)]
    specs = [SCALAR] + [VMEM] * 6
    out = state_of(GROUP) + state_of(HALF_HEADS)
    outs = call(here_kernel, "here_keys", specs, out, scratch, 3 * HALF_HEADS * ROWS, PAIR)(
        place, q, q_rows, *state, here, other
    )
    return outs[:2], outs[2:]


def attend_last(place, tree, length, q, state, q_rows, state_rows, held, k_own, v_own):
    specs = [SCALAR] * 3 + [VMEM] * (6 + len(held)) + [ANYWHERE] * (2 + len(held))
    scratch = KEYS + [
        pltpu.VMEM((1, ROWS), jnp.float32),
        pltpu.VMEM((1, ROWS), jnp.float32),
        pltpu.VMEM((2, HD, HD), jnp.bfloat16),
        pltpu.VMEM((2, ROWS, HD), jnp.bfloat16),
    ]
    scratch += KEYS + [
        pltpu.VMEM((PAIR, ROWS), jnp.float32),
        pltpu.VMEM((HALF_HEADS, HD, ROWS), jnp.float32),
        pltpu.VMEM((HALF_HEADS, 8, ROWS), jnp.float32),
        pltpu.VMEM((HALF_HEADS, 1, ROWS), jnp.float32),
    ]
    out = (
        jax.ShapeDtypeStruct((ROWS, GROUP * HD), jnp.bfloat16),
        jax.ShapeDtypeStruct(q_rows.shape, jnp.bfloat16),
    )
    return call(last_kernel, "last_keys", specs, out, scratch, 2 * GROUP * ROWS, PAIR)(
        place, tree, length, q, *state, q_rows, *state_rows, *held, k_own, v_own, *held
    )


def after(value, *events):
    return lax.optimization_barrier((value, *events))[0]


def on_device(q_prompt, k_prompt, v_prompt, q_resp, k_resp, v_resp, tree_table, lengths):
    chain, resp = lax.axis_index("chain"), lax.axis_index("resp")
    y, z, x, core = chain // 2, chain % 2 * 2 + resp // 2 % 2, resp // 4, resp % 2
    place = jnp.stack([y, z, x, core]).astype(jnp.int32)
    q = q_resp[0]

    def cols(block, at, count):
        return lax.dynamic_slice_in_dim(block, at * count * HD, count * HD, block.ndim - 1)

    own = jnp.stack([k_prompt, v_prompt])
    over = pick(place, own, move(k_prompt, other_core), move(v_prompt, other_core))
    over = [over[0]] + [move(part, first_axis(d)) for part, d in zip(over[1:], STEPS[1:])]
    over = jnp.stack(over)

    def for_z(at):
        return cols(over, jnp.where(core == 0, at // 2, at % 2), 1)

    over_z = [for_z(z)] + [move(for_z((z + d) % 4), along_z(d)) for d in STEPS[1:]]
    state = attend_own(tree_table, lengths, after(q, over), k_resp[0], v_resp[0])
    here = arrange(after(over_z, state[1]))
    here_o = move(here, other_core)
    left, right = move(here, last_axis(1)), move(here, last_axis(3))
    state, prompt_state = attend_here(place, q, q_prompt, state, here, here_o)
    left, right = after((left, right), state[1], prompt_state[1])
    left_o, right_o = move(left, other_core), move(right, other_core)
    far_l, far_r = move(left[:4], last_axis(1)), move(right[4:], last_axis(3))
    state = attend_chunk(place, q, state, left, left_o, "left_keys")
    far_l, far_r = after((far_l, far_r), state[1])
    far = jnp.concatenate([far_l, far_r])
    far_o = move(far, other_core)
    state = attend_chunk(place, q, state, right, right_o, "right_keys")
    held = (here, left, right, far, here_o, left_o, right_o, far_o)
    resp_out, prompt_out = attend_last(
        place, tree_table, lengths, q, state, q_prompt, prompt_state, held, k_resp[0], v_resp[0]
    )
    return (prompt_out, resp_out[None])


def solution(mesh):
    placed = (
        P("chain", "resp"),
        P(("chain", "resp"), None),
        P(("chain", "resp"), None),
        P("resp", None, "chain"),
        P("resp", None, "chain"),
        P("resp", None, "chain"),
        P("resp", None),
        P("resp"),
    )
    return jax.shard_map(
        on_device,
        mesh=mesh,
        in_specs=placed,
        out_specs=(P("chain", "resp"), P("resp", None, "chain")),
        check_vma=False,
    )
```

```python
import functools

import jax
import jax.numpy as jnp
from jax import lax
from jax.experimental import pallas as pl
from jax.experimental.pallas import tpu as pltpu
from jax.sharding import PartitionSpec as P

QH = 64
KVH = 8
HD = 128
RBLK = 8
ROWS = 512
SUB = 32
GROUP = QH // KVH
STEP_HEADS = 4
SCALE = HD**-0.5 * 1.4426950408889634
LOW, HIGH = 1e-18, 1e30
AXES = ("chain", "resp")
STEPS = (0, 1, 3, 2)
CHUNKS = 4
MIB = 2**20
PLACES = [(y, z, x, k) for y in range(4) for z in range(4) for x in range(4) for k in range(2)]


def device_at(y, z, x, core):
    return (y * 2 + z // 2) * 16 + (x * 2 + z % 2) * 2 + core


def move(block, target):
    route = [(device_at(*p), device_at(*target(*p))) for p in PLACES]
    return lax.ppermute(block, AXES, route)


def first_axis(d):
    def target(y, z, x, core):
        return (y, z, (x + d) % 4, core) if core else ((y + d) % 4, z, x, core)

    return target


def along_z(d):
    return lambda y, z, x, core: (y, (z + d) % 4, x, core)


def last_axis(d):
    def target(y, z, x, core):
        return ((y + d) % 4, z, x, core) if core else (y, z, (x + d) % 4, core)

    return target


def other_core(y, z, x, core):
    return (y, z, x, 1 - core)


def coordinates():
    chain, resp = lax.axis_index("chain"), lax.axis_index("resp")
    return chain // 2, chain % 2 * 2 + resp // 2 % 2, resp // 4, resp % 2


def dot_t(a, b):
    return lax.dot_general(a, b, (((1,), (1,)), ((), ())), preferred_element_type=jnp.float32)


def fold_rows(p):
    return jnp.sum(p.reshape(p.shape[0] // 8, 8, p.shape[1]), axis=0)


def online(carried, keys, values_t, queries, visible):
    run_max, run_sum, run_acc = carried
    scores = dot_t(keys, queries) * SCALE
    if visible is not None:
        scores = jnp.where(visible, scores, -1e30)
    new_max = jnp.maximum(run_max, jnp.max(scores, axis=0, keepdims=True))
    weights = jnp.exp2(scores - new_max)
    if visible is not None:
        weights = jnp.where(visible, weights, 0.0)
    rescale = jnp.exp2(run_max - new_max)
    run_sum = run_sum * rescale + jnp.sum(weights, axis=0, keepdims=True)
    added = jnp.dot(values_t, weights.astype(jnp.bfloat16), preferred_element_type=jnp.float32)
    return (new_max, run_sum, run_acc * rescale + added)


def fresh(cols):
    return (
        jnp.full((1, cols), -1e30, jnp.float32),
        jnp.zeros((1, cols), jnp.float32),
        jnp.zeros((HD, cols), jnp.float32),
    )


def tree_seen(tree_ref, len_ref):
    lines = []
    for j in range(RBLK):
        parent = tree_ref[0, j]
        line = jnp.int32(1 << j)
        for i in range(j):
            line = line | jnp.where(parent == i, lines[i], 0)
        lines.append(line)
    key_at = lax.broadcasted_iota(jnp.int32, (ROWS, ROWS), 0)
    row_at = lax.broadcasted_iota(jnp.int32, (ROWS, ROWS), 1)
    span = ROWS // RBLK
    line_of_row = jnp.zeros((ROWS, ROWS), jnp.int32)
    for j in range(RBLK):
        line_of_row = jnp.where(row_at // span == j, lines[j], line_of_row)
    related = (lax.shift_right_logical(line_of_row, key_at // span) & 1) == 1
    return related & (key_at <= row_at) & (key_at < len_ref[0])


def weigh(keys, queries, values_t, shown=None):
    scores = dot_t(keys, queries) * SCALE
    weights = jnp.exp2(scores if shown is None else scores + shown)
    added = jnp.dot(values_t, weights.astype(jnp.bfloat16), preferred_element_type=jnp.float32)
    return fold_rows(weights), added


def over_heads(one_head):
    def some(step, unused):
        for h in range(STEP_HEADS):
            head = step * STEP_HEADS + h
            one_head(head, pl.ds(pl.multiple_of(head * HD, HD), HD))
        return unused

    lax.fori_loop(0, GROUP // STEP_HEADS, some, 0)


def own_kernel(tree_ref, len_ref, q_ref, k_ref, v_ref, acc_ref, sum_ref, seen, live, vt):
    vt[...] = v_ref[...].T
    rows = lax.broadcasted_iota(jnp.int32, live.shape, 1)
    live[...] = jnp.where(rows < len_ref[0], 1.0, 0.0)
    seen[...] = jnp.where(tree_seen(tree_ref, len_ref), 0.0, -jnp.inf)

    def one_head(h, cols):
        sum_ref[h], acc_ref[h] = weigh(k_ref[...], q_ref[:, cols], vt[...], seen[...])

    over_heads(one_head)


def pick_kernel(own, k_other, v_other, *outs):
    y, z, x, core = coordinates()
    near = jnp.where(core == 0, y, x)
    for step, out_ref in zip(STEPS, outs):
        width = 2 * HD
        cols = pl.ds(pl.multiple_of((near + step) % 4 * width, width), width)
        for i, other in enumerate((k_other, v_other)):
            out_ref[i, :SUB, :] = own[i, :, cols]
            out_ref[i, SUB:, :] = other[:, cols]


def arrange_kernel(*refs):
    out_ref = refs[4]
    for i, ref in enumerate(refs[:4]):
        for half in range(2):
            pieces = ref[2 * half : 2 * half + 2]
            out_ref[2 * i + half, 0] = pieces[:, 0].reshape(HD, HD)
            out_ref[2 * i + half, 1] = pieces[:, 1].reshape(HD, HD).T


def load_blocks(chunk, kb, vt):
    for b in range(8):
        kb[b * HD : (b + 1) * HD, :] = chunk[b, 0]
        vt[:, b * HD : (b + 1) * HD] = chunk[b, 1]


def load_chunk(role, here, other, kb, vt):
    core = coordinates()[3]

    @pl.when(core == role)
    def _():
        load_blocks(here, kb, vt)

    @pl.when(core != role)
    def _():
        load_blocks(other, kb, vt)


def load_sides(role, left, left_o, right, right_o, kb, vt):
    load_chunk(role, left, left_o, kb.at[:PAIR], vt.at[:, :PAIR])
    load_chunk(role, right, right_o, kb.at[PAIR:], vt.at[:, PAIR:])


def wide_kernel(q_ref, acc_in, sum_in, left, left_o, right, right_o, acc_ref, sum_ref, kb, vt):
    load_sides(0, left, left_o, right, right_o, kb, vt)
    add_heads(q_ref, acc_in, sum_in, acc_ref, sum_ref, kb, vt)


def add_heads(q_ref, acc_in, sum_in, acc_ref, sum_ref, kb, vt):
    def one_head(h, cols):
        sums, accs = weigh(kb[...], q_ref[:, cols], vt[...])
        sum_ref[h] = sum_in[h] + sums
        acc_ref[h] = acc_in[h] + accs

    over_heads(one_head)


def in_range(low, high):
    return (jnp.min(low) > LOW) & (jnp.max(high) < HIGH)


def side_kernel(q_ref, acc_in, sum_in, left, left_o, right, right_o, acc_ref, sum_ref, kb, vt):
    y = coordinates()[0]
    load_sides(1, left, left_o, right, right_o, kb, vt)

    def add(count):
        for h in range(HALF_HEADS):
            queries = q_ref[:, h * HD : (h + 1) * HD]
            sums, accs = weigh(kb[:count], queries, vt[:, :count])
            sum_ref[h] = sum_in[h] + sums
            acc_ref[h] = acc_in[h] + accs

    @pl.when(y == 3)
    def _():
        add(2 * PAIR)

    @pl.when((y == 1) | (y == 2))
    def _():
        add(PAIR)

    @pl.when(y == 0)
    def _():
        sum_ref[...] = sum_in[...]
        acc_ref[...] = acc_in[...]


def prompt_part(q_ref, acc_in, sum_in, held, out_ref, kb, vt, seen, acc, total, top):
    y = coordinates()[0]

    def queries(h):
        return q_ref[:, h * HD : (h + 1) * HD]

    @pl.when(y >= 2)
    def _():
        load_chunk(1, held[3], held[CHUNKS + 3], kb, vt)
        for h in range(HALF_HEADS):
            sums, accs = weigh(kb[...], queries(h), vt[...])
            total[h] = sum_in[h] + sums
            acc[h] = acc_in[h] + accs

    @pl.when(y < 2)
    def _():
        total[...] = sum_in[...]
        acc[...] = acc_in[...]

    def store(h, sums):
        shown = (acc[h] * (1.0 / sums)).astype(jnp.bfloat16)
        out_ref[:, h * HD : (h + 1) * HD] = shown.T

    low = high = jnp.ones((1, ROWS), jnp.float32)
    for h in range(HALF_HEADS):
        sums = jnp.sum(total[h], axis=0, keepdims=True)
        store(h, sums)
        low, high = jnp.minimum(low, sums), jnp.maximum(high, sums)

    @pl.when(jnp.logical_not(in_range(low, high)))
    def _():
        load_chunk(1, held[0], held[CHUNKS], kb, vt)
        for rows, visible in own_pair_seen():
            seen[rows, :] = jnp.where(visible, 1.0, 0.0)
        top[...] = jnp.full_like(top, -1e30)
        total[...] = jnp.zeros_like(total)
        acc[...] = jnp.zeros_like(acc)

        def exact():
            def one_head(h, unused):
                cols = pl.ds(pl.multiple_of(h * HD, HD), HD)
                carried = (top[h], total[h, 0:1], acc[h])
                carried = online(carried, kb[...], vt[...], q_ref[:, cols], seen[...] > 0.5)
                top[h], total[h, 0:1], acc[h] = carried
                return unused

            lax.fori_loop(0, HALF_HEADS, one_head, 0)

        exact()
        seen[...] = jnp.ones_like(seen)

        def one_pair(i, unused):
            for at, spot in enumerate((1, 3, 2)):

                @pl.when(i == at)
                def _(spot=spot):
                    load_chunk(1, held[spot], held[CHUNKS + spot], kb, vt)

            exact()
            return unused

        lax.fori_loop(0, y, one_pair, 0)
        for h in range(HALF_HEADS):
            store(h, total[h, 0:1])


def last_kernel(q_ref, acc_in, sum_in, live_ref, *refs):
    q_rows, acc_rows, sum_rows = refs[:3]
    rows_held, (k_own, v_own, seen_own), refs = refs[3 : 3 + 2 * CHUNKS], refs[11:14], refs[14:]
    held, refs = refs[: 2 * CHUNKS], refs[2 * CHUNKS :]
    out_ref, out_rows, kb, vt, low, high, block, own = refs[:8]
    prompt_part(q_rows, acc_rows, sum_rows, rows_held, out_rows, *refs[8:])
    is_first = coordinates()[3] == 0
    load_chunk(0, rows_held[CHUNKS - 1], rows_held[2 * CHUNKS - 1], kb, vt)
    low[...] = jnp.full_like(low, 1.0)
    high[...] = jnp.full_like(high, 1.0)
    live = live_ref[0:1] > 0.5

    def store(cols, acc, total):
        shown = jnp.where(live, acc * (1.0 / total), 0.0)
        out_ref[:, cols] = shown.astype(jnp.bfloat16).T

    def one_head(h, cols):
        sums, accs = weigh(kb[...], q_ref[:, cols], vt[...])
        total = jnp.sum(sum_in[h] + sums, axis=0, keepdims=True)
        low[...] = jnp.minimum(low[...], total)
        high[...] = jnp.maximum(high[...], total)
        store(cols, acc_in[h] + accs, total)

    over_heads(one_head)

    @pl.when(jnp.logical_not(in_range(low[...], high[...])))
    def _():
        pltpu.sync_copy(k_own, own.at[0])
        pltpu.sync_copy(v_own, own.at[1])
        seen_buf = refs[10].at[:ROWS]
        pltpu.sync_copy(seen_own, seen_buf)

        def exact_head(h, unused):
            cols = pl.ds(pl.multiple_of(h * HD, HD), HD)
            queries = q_ref[:, cols]

            def one_block(i, carried, one, two):
                @pl.when(is_first)
                def _():
                    pltpu.sync_copy(one.at[i], block)

                @pl.when(jnp.logical_not(is_first))
                def _():
                    pltpu.sync_copy(two.at[i], block)

                return online(carried, block[0], block[1], queries, None)

            carried = fresh(ROWS)
            for one, two in zip(held[:CHUNKS], held[CHUNKS:]):
                carried = lax.fori_loop(
                    0, 8, functools.partial(one_block, one=one, two=two), carried
                )
            visible = seen_buf[...] > -1.0
            run_max, run_sum, run_acc = online(carried, own[0], own[1].T, queries, visible)
            store(cols, run_acc, run_sum)
            return unused

        lax.fori_loop(0, GROUP, exact_head, 0)


def own_pair_seen():
    y, z, x, core = coordinates()
    row_at = lax.broadcasted_iota(jnp.int32, (SUB, ROWS), 1) + z // 2 * ROWS
    key_at = lax.broadcasted_iota(jnp.int32, (SUB, ROWS), 0)
    for i, z_step in enumerate(STEPS):
        for j, x_step in enumerate(STEPS):
            x0, z0 = (x - x_step) % 4, (z - z_step) % 4
            for lane in range(2):
                first = (z0 // 2) * ROWS + ((x0 * 2 + z0 % 2) * 2 + 1 - lane) * SUB
                at = ((i * 4 + j) * 2 + lane) * SUB
                yield slice(at, at + SUB), key_at + first <= row_at


def here_kernel(q_ref, q_rows, acc_in, sum_in, here, other, *refs):
    acc_ref, sum_ref, acc_rows, sum_rows, kb, vt, kb_rows, vt_rows, seen = refs
    load_chunk(0, here, other, kb, vt)
    add_heads(q_ref, acc_in, sum_in, acc_ref, sum_ref, kb, vt)
    load_chunk(1, here, other, kb_rows, vt_rows)
    for rows, visible in own_pair_seen():
        seen[rows, :] = jnp.where(visible, 0.0, -jnp.inf)
    for h in range(HALF_HEADS):
        queries = q_rows[:, h * HD : (h + 1) * HD]
        sum_rows[h], acc_rows[h] = weigh(kb_rows[...], queries, vt_rows[...], seen[...])


HALF_HEADS = GROUP // 2
PAIR = 2 * ROWS
CHUNK = jax.ShapeDtypeStruct((8, 2, HD, HD), jnp.bfloat16)


def state_of(heads):
    return (
        jax.ShapeDtypeStruct((heads, HD, ROWS), jnp.float32),
        jax.ShapeDtypeStruct((heads, 8, ROWS), jnp.float32),
    )


SCALAR = pl.BlockSpec(memory_space=pltpu.SMEM)
VMEM = pl.BlockSpec(memory_space=pltpu.VMEM)
ANYWHERE = pl.BlockSpec(memory_space=pl.ANY)


def keys_of(count):
    return [pltpu.VMEM((count, HD), jnp.bfloat16), pltpu.VMEM((HD, count), jnp.bfloat16)]


KEYS = keys_of(PAIR)


def call(kernel, name, in_specs, out_shape, scratch, rows, keys):
    single = not isinstance(out_shape, tuple)
    return pl.pallas_call(
        kernel,
        in_specs=in_specs,
        out_specs=VMEM if single else tuple(VMEM for _ in out_shape),
        out_shape=out_shape,
        scratch_shapes=scratch,
        cost_estimate=pl.CostEstimate(
            flops=8 * rows * keys * HD, bytes_accessed=6 * MIB, transcendentals=rows * keys
        ),
        compiler_params=pltpu.CompilerParams(vmem_limit_bytes=32 * MIB),
        name=name,
    )


def attend_own(tree, length, q, k, v):
    scratch = [pltpu.VMEM((HD, ROWS), jnp.bfloat16)]
    specs = [SCALAR, SCALAR, VMEM, VMEM, VMEM]
    out = state_of(GROUP) + (
        jax.ShapeDtypeStruct((ROWS, ROWS), jnp.float32),
        jax.ShapeDtypeStruct((8, ROWS), jnp.float32),
    )
    outs = call(own_kernel, "own_keys", specs, out, scratch, GROUP * ROWS, ROWS)(
        tree, length, q, k, v
    )
    return outs[:2], outs[2], outs[3]


def pick(own, k_other, v_other):
    out = tuple(jax.ShapeDtypeStruct((2, 2 * SUB, 2 * HD), jnp.bfloat16) for _ in STEPS)
    return call(pick_kernel, "pick", [VMEM] * 3, out, [], 8, 8)(own, k_other, v_other)


def arrange(parts):
    return call(arrange_kernel, "arrange", [VMEM] * 4, CHUNK, [], 8, 8)(*parts)


def attend_here(q, q_rows, state, here, other):
    scratch = KEYS + KEYS + [pltpu.VMEM((PAIR, ROWS), jnp.float32)]
    out = state_of(GROUP) + state_of(HALF_HEADS)
    outs = call(here_kernel, "here_keys", [VMEM] * 6, out, scratch, 3 * HALF_HEADS * ROWS, PAIR)(
        q, q_rows, *state, here, other
    )
    return outs[:2], outs[2:]


def attend_sides(kernel, name, heads, q, state, sides):
    scratch = keys_of(2 * PAIR)
    return call(kernel, name, [VMEM] * 7, state_of(heads), scratch, heads * ROWS, 2 * PAIR)(
        q, *state, *sides
    )


def attend_last(q, state, live, q_rows, state_rows, held, k_own, v_own, seen):
    specs = [VMEM] * (7 + len(held)) + [ANYWHERE] * (3 + len(held))
    scratch = KEYS + [
        pltpu.VMEM((1, ROWS), jnp.float32),
        pltpu.VMEM((1, ROWS), jnp.float32),
        pltpu.VMEM((2, HD, HD), jnp.bfloat16),
        pltpu.VMEM((2, ROWS, HD), jnp.bfloat16),
    ]
    scratch += KEYS + [
        pltpu.VMEM((PAIR, ROWS), jnp.float32),
        pltpu.VMEM((HALF_HEADS, HD, ROWS), jnp.float32),
        pltpu.VMEM((HALF_HEADS, 8, ROWS), jnp.float32),
        pltpu.VMEM((HALF_HEADS, 1, ROWS), jnp.float32),
    ]
    out = (
        jax.ShapeDtypeStruct((ROWS, GROUP * HD), jnp.bfloat16),
        jax.ShapeDtypeStruct(q_rows.shape, jnp.bfloat16),
    )
    return call(last_kernel, "last_keys", specs, out, scratch, 2 * GROUP * ROWS, PAIR)(
        q, *state, live, q_rows, *state_rows, *held, k_own, v_own, seen, *held
    )


def after(value, *events):
    return lax.optimization_barrier((value, *events))[0]


def on_device(q_prompt, k_prompt, v_prompt, q_resp, k_resp, v_resp, tree_table, lengths):
    y, z, x, core = coordinates()
    q = q_resp[0]

    def cols(block, at, count):
        return lax.dynamic_slice_in_dim(block, at * count * HD, count * HD, block.ndim - 1)

    own = jnp.stack([k_prompt, v_prompt])
    over = pick(own, move(k_prompt, other_core), move(v_prompt, other_core))
    over = [over[0]] + [move(part, first_axis(d)) for part, d in zip(over[1:], STEPS[1:])]
    over = jnp.stack(over)

    def for_z(at):
        return cols(over, jnp.where(core == 0, at // 2, at % 2), 1)

    over_z = [for_z(z)] + [move(for_z((z + d) % 4), along_z(d)) for d in STEPS[1:]]
    q = after(q, over)
    state, seen, live = attend_own(tree_table, lengths, q, k_resp[0], v_resp[0])
    over_z = after(over_z, live)
    here = arrange(over_z)
    here_o = move(here, other_core)
    left, right = move(here, last_axis(1)), move(here, last_axis(3))
    state, rows_state = attend_here(q, q_prompt, state, here, here_o)
    left, right = after((left, right), state[1])
    left_o, right_o = move(left, other_core), move(right, other_core)
    far_l, far_r = move(left[:4], last_axis(1)), move(right[4:], last_axis(3))
    sides = (left, left_o, right, right_o)
    state = attend_sides(wide_kernel, "wide_keys", GROUP, q, state, sides)
    far_l, far_r = after((far_l, far_r), state[1])
    far = jnp.concatenate([far_l, far_r])
    far_o = move(far, other_core)
    rows_state = attend_sides(side_kernel, "side_rows", HALF_HEADS, q_prompt, rows_state, sides)
    held = (here, left, right, far, here_o, left_o, right_o, after(far_o, rows_state[1]))
    resp_out, prompt_out = attend_last(
        q, state, live, q_prompt, rows_state, held, k_resp[0], v_resp[0], seen
    )
    return (prompt_out, resp_out[None])


def solution(mesh):
    placed = (
        P("chain", "resp"),
        P(("chain", "resp"), None),
        P(("chain", "resp"), None),
        P("resp", None, "chain"),
        P("resp", None, "chain"),
        P("resp", None, "chain"),
        P("resp", None),
        P("resp"),
    )
    return jax.shard_map(
        on_device,
        mesh=mesh,
        in_specs=placed,
        out_specs=(P("chain", "resp"), P("resp", None, "chain")),
        check_vma=False,
    )
```

```python
import functools

import jax
import jax.numpy as jnp
from jax import lax
from jax.experimental import pallas as pl
from jax.experimental.pallas import tpu as pltpu
from jax.sharding import PartitionSpec as P

QH = 64
KVH = 8
HD = 128
RBLK = 8
ROWS = 512
SUB = 32
GROUP = QH // KVH
STEP_HEADS = 4
SCALE = HD**-0.5 * 1.4426950408889634
LOW, HIGH = 1e-18, 1e30
AXES = ("chain", "resp")
STEPS = (0, 1, 3, 2)
CHUNKS = 4
MIB = 2**20
PLACES = [(y, z, x, k) for y in range(4) for z in range(4) for x in range(4) for k in range(2)]


def device_at(y, z, x, core):
    return (y * 2 + z // 2) * 16 + (x * 2 + z % 2) * 2 + core


def move(block, target):
    route = [(device_at(*p), device_at(*target(*p))) for p in PLACES]
    return lax.ppermute(block, AXES, route)


def first_axis(d):
    def target(y, z, x, core):
        return (y, z, (x + d) % 4, core) if core else ((y + d) % 4, z, x, core)

    return target


def along_z(d):
    return lambda y, z, x, core: (y, (z + d) % 4, x, core)


def last_axis(d):
    def target(y, z, x, core):
        return ((y + d) % 4, z, x, core) if core else (y, z, (x + d) % 4, core)

    return target


def other_core(y, z, x, core):
    return (y, z, x, 1 - core)


def coordinates():
    chain, resp = lax.axis_index("chain"), lax.axis_index("resp")
    return chain // 2, chain % 2 * 2 + resp // 2 % 2, resp // 4, resp % 2


def dot_t(a, b):
    return lax.dot_general(a, b, (((1,), (1,)), ((), ())), preferred_element_type=jnp.float32)


def fold_rows(p):
    return jnp.sum(p.reshape(p.shape[0] // 8, 8, p.shape[1]), axis=0)


def online(carried, keys, values_t, queries, visible):
    run_max, run_sum, run_acc = carried
    scores = dot_t(keys, queries) * SCALE
    if visible is not None:
        scores = jnp.where(visible, scores, -1e30)
    new_max = jnp.maximum(run_max, jnp.max(scores, axis=0, keepdims=True))
    weights = jnp.exp2(scores - new_max)
    if visible is not None:
        weights = jnp.where(visible, weights, 0.0)
    rescale = jnp.exp2(run_max - new_max)
    run_sum = run_sum * rescale + jnp.sum(weights, axis=0, keepdims=True)
    added = jnp.dot(values_t, weights.astype(jnp.bfloat16), preferred_element_type=jnp.float32)
    return (new_max, run_sum, run_acc * rescale + added)


def fresh(cols):
    return (
        jnp.full((1, cols), -1e30, jnp.float32),
        jnp.zeros((1, cols), jnp.float32),
        jnp.zeros((HD, cols), jnp.float32),
    )


def tree_seen(tree_ref, len_ref):
    lines = []
    for j in range(RBLK):
        parent = tree_ref[0, j]
        line = jnp.int32(1 << j)
        for i in range(j):
            line = line | jnp.where(parent == i, lines[i], 0)
        lines.append(line)
    key_at = lax.broadcasted_iota(jnp.int32, (ROWS, ROWS), 0)
    row_at = lax.broadcasted_iota(jnp.int32, (ROWS, ROWS), 1)
    span = ROWS // RBLK
    line_of_row = jnp.zeros((ROWS, ROWS), jnp.int32)
    for j in range(RBLK):
        line_of_row = jnp.where(row_at // span == j, lines[j], line_of_row)
    related = (lax.shift_right_logical(line_of_row, key_at // span) & 1) == 1
    return related & (key_at <= row_at) & (key_at < len_ref[0])


def weigh(keys, queries, values_t, shown=None):
    scores = dot_t(keys, queries) * SCALE
    weights = jnp.exp2(scores if shown is None else scores + shown)
    added = jnp.dot(values_t, weights.astype(jnp.bfloat16), preferred_element_type=jnp.float32)
    return fold_rows(weights), added


def weigh_pair(keys, q_ref, h, values_t, shown=None):
    queries = jnp.concatenate([q_ref[:, (h + i) * HD : (h + i + 1) * HD] for i in range(2)])
    if shown is not None:
        shown = jnp.concatenate([shown, shown], 1)
    sums, accs = weigh(keys, queries, values_t, shown)
    for i in range(2):
        yield h + i, sums[:, i * ROWS : (i + 1) * ROWS], accs[:, i * ROWS : (i + 1) * ROWS]


def over_heads(one_head):
    def some(step, unused):
        for h in range(STEP_HEADS):
            head = step * STEP_HEADS + h
            one_head(head, pl.ds(pl.multiple_of(head * HD, HD), HD))
        return unused

    lax.fori_loop(0, GROUP // STEP_HEADS, some, 0)


def own_kernel(tree_ref, len_ref, q_ref, k_ref, v_ref, acc_ref, sum_ref, seen, live, vt):
    vt[...] = v_ref[...].T
    rows = lax.broadcasted_iota(jnp.int32, live.shape, 1)
    live[...] = jnp.where(rows < len_ref[0], 1.0, 0.0)
    seen[...] = jnp.where(tree_seen(tree_ref, len_ref), 0.0, -jnp.inf)

    def one_head(h, cols):
        sum_ref[h], acc_ref[h] = weigh(k_ref[...], q_ref[:, cols], vt[...], seen[...])

    over_heads(one_head)


def pick_kernel(own, k_other, v_other, *outs):
    y, z, x, core = coordinates()
    near = jnp.where(core == 0, y, x)
    for step, out_ref in zip(STEPS, outs):
        width = 2 * HD
        cols = pl.ds(pl.multiple_of((near + step) % 4 * width, width), width)
        for i, other in enumerate((k_other, v_other)):
            out_ref[i, :SUB, :] = own[i, :, cols]
            out_ref[i, SUB:, :] = other[:, cols]


def arrange_kernel(*refs):
    out_ref = refs[4]
    for i, ref in enumerate(refs[:4]):
        for half in range(2):
            pieces = ref[2 * half : 2 * half + 2]
            out_ref[2 * i + half, 0] = pieces[:, 0].reshape(HD, HD)
            out_ref[2 * i + half, 1] = pieces[:, 1].reshape(HD, HD).T


def load_blocks(chunk, kb, vt):
    for b in range(8):
        kb[b * HD : (b + 1) * HD, :] = chunk[b, 0]
        vt[:, b * HD : (b + 1) * HD] = chunk[b, 1]


def load_chunk(role, here, other, kb, vt):
    core = coordinates()[3]

    @pl.when(core == role)
    def _():
        load_blocks(here, kb, vt)

    @pl.when(core != role)
    def _():
        load_blocks(other, kb, vt)


def load_sides(role, left, left_o, right, right_o, kb, vt):
    load_chunk(role, left, left_o, kb.at[:PAIR], vt.at[:, :PAIR])
    load_chunk(role, right, right_o, kb.at[PAIR:], vt.at[:, PAIR:])


def wide_kernel(q_ref, acc_in, sum_in, left, left_o, right, right_o, acc_ref, sum_ref, kb, vt):
    load_sides(0, left, left_o, right, right_o, kb, vt)
    add_heads(q_ref, acc_in, sum_in, acc_ref, sum_ref, kb, vt)


def add_heads(q_ref, acc_in, sum_in, acc_ref, sum_ref, kb, vt):
    def one_head(h, cols):
        sums, accs = weigh(kb[...], q_ref[:, cols], vt[...])
        sum_ref[h] = sum_in[h] + sums
        acc_ref[h] = acc_in[h] + accs

    over_heads(one_head)


def in_range(low, high):
    return (jnp.min(low) > LOW) & (jnp.max(high) < HIGH)


def side_kernel(q_ref, acc_in, sum_in, left, left_o, right, right_o, acc_ref, sum_ref, kb, vt):
    y = coordinates()[0]
    load_sides(1, left, left_o, right, right_o, kb, vt)

    def add(count):
        for h in range(HALF_HEADS):
            queries = q_ref[:, h * HD : (h + 1) * HD]
            sums, accs = weigh(kb[:count], queries, vt[:, :count])
            sum_ref[h] = sum_in[h] + sums
            acc_ref[h] = acc_in[h] + accs

    @pl.when(y == 3)
    def _():
        add(2 * PAIR)

    @pl.when((y == 1) | (y == 2))
    def _():
        add(PAIR)

    @pl.when(y == 0)
    def _():
        sum_ref[...] = sum_in[...]
        acc_ref[...] = acc_in[...]


def prompt_part(q_ref, acc_in, sum_in, held, out_ref, put, kb, vt, seen, acc, total, top):
    y = coordinates()[0]

    def queries(h):
        return q_ref[:, h * HD : (h + 1) * HD]

    @pl.when(y >= 2)
    def _():
        load_chunk(1, held[3], held[CHUNKS + 3], kb, vt)
        for pair in range(0, HALF_HEADS, 2):
            for h, sums, accs in weigh_pair(kb[...], q_ref, pair, vt[...]):
                total[h] = sum_in[h] + sums
                acc[h] = acc_in[h] + accs

    @pl.when(y < 2)
    def _():
        total[...] = sum_in[...]
        acc[...] = acc_in[...]

    def store(h, sums):
        shown = (acc[h] * (1.0 / sums)).astype(jnp.bfloat16)
        out_ref[:, h * HD : (h + 1) * HD] = shown.T

    low = high = jnp.ones((1, ROWS), jnp.float32)
    for h in range(HALF_HEADS):
        sums = jnp.sum(total[h], axis=0, keepdims=True)
        store(h, sums)
        low, high = jnp.minimum(low, sums), jnp.maximum(high, sums)
    put.start()

    def exact_rows():
        load_chunk(1, held[0], held[CHUNKS], kb, vt)
        for rows, visible in own_pair_seen():
            seen[rows, :] = jnp.where(visible, 1.0, 0.0)
        top[...] = jnp.full_like(top, -1e30)
        total[...] = jnp.zeros_like(total)
        acc[...] = jnp.zeros_like(acc)

        def exact():
            def one_head(h, unused):
                cols = pl.ds(pl.multiple_of(h * HD, HD), HD)
                carried = (top[h], total[h, 0:1], acc[h])
                carried = online(carried, kb[...], vt[...], q_ref[:, cols], seen[...] > 0.5)
                top[h], total[h, 0:1], acc[h] = carried
                return unused

            lax.fori_loop(0, HALF_HEADS, one_head, 0)

        exact()
        seen[...] = jnp.ones_like(seen)

        def one_pair(i, unused):
            for at, spot in enumerate((1, 3, 2)):

                @pl.when(i == at)
                def _(spot=spot):
                    load_chunk(1, held[spot], held[CHUNKS + spot], kb, vt)

            exact()
            return unused

        lax.fori_loop(0, y, one_pair, 0)
        for h in range(HALF_HEADS):
            store(h, total[h, 0:1])
        put.start()
        put.wait()

    return low, high, exact_rows


def last_kernel(q_ref, acc_in, sum_in, live_ref, *refs):
    q_rows, acc_rows, sum_rows = refs[:3]
    rows_held, (k_own, v_own, seen_own), refs = refs[3 : 3 + 2 * CHUNKS], refs[11:14], refs[14:]
    held, refs = refs[: 2 * CHUNKS], refs[2 * CHUNKS :]
    out_hbm, rows_hbm, out_ref, out_rows, done, kb, vt, low, high, block, own = refs[:11]
    put_rows = pltpu.make_async_copy(out_rows, rows_hbm, done.at[GROUP])
    low[...], high[...], exact_rows = prompt_part(
        q_rows, acc_rows, sum_rows, rows_held, out_rows, put_rows, *refs[11:]
    )

    def put(h, cols):
        return pltpu.make_async_copy(out_ref.at[:, cols], out_hbm.at[:, cols], done.at[h])

    is_first = coordinates()[3] == 0
    load_chunk(0, rows_held[CHUNKS - 1], rows_held[2 * CHUNKS - 1], kb, vt)
    live = live_ref[0:1] > 0.5

    def store(cols, acc, total):
        shown = jnp.where(live, acc * (1.0 / total), 0.0)
        out_ref[:, cols] = shown.astype(jnp.bfloat16).T

    for pair in range(0, GROUP, 2):
        for h, sums, accs in weigh_pair(kb[...], q_ref, pair, vt[...]):
            total = jnp.sum(sum_in[h] + sums, axis=0, keepdims=True)
            low[...] = jnp.minimum(low[...], total)
            high[...] = jnp.maximum(high[...], total)
            cols = slice(h * HD, (h + 1) * HD)
            store(cols, acc_in[h] + accs, total)
            put(h, cols).start()
    put_rows.wait()
    for h in range(GROUP):
        put(h, slice(h * HD, (h + 1) * HD)).wait()

    @pl.when(jnp.logical_not(in_range(low[...], high[...])))
    def _():
        pltpu.sync_copy(k_own, own.at[0])
        pltpu.sync_copy(v_own, own.at[1])
        exact_rows()
        seen_buf = refs[13].at[:ROWS]
        pltpu.sync_copy(seen_own, seen_buf)

        def exact_head(h, unused):
            cols = pl.ds(pl.multiple_of(h * HD, HD), HD)
            queries = q_ref[:, cols]

            def one_block(i, carried, one, two):
                @pl.when(is_first)
                def _():
                    pltpu.sync_copy(one.at[i], block)

                @pl.when(jnp.logical_not(is_first))
                def _():
                    pltpu.sync_copy(two.at[i], block)

                return online(carried, block[0], block[1], queries, None)

            carried = fresh(ROWS)
            for one, two in zip(held[:CHUNKS], held[CHUNKS:]):
                carried = lax.fori_loop(
                    0, 8, functools.partial(one_block, one=one, two=two), carried
                )
            visible = seen_buf[...] > -1.0
            run_max, run_sum, run_acc = online(carried, own[0], own[1].T, queries, visible)
            store(cols, run_acc, run_sum)
            put(h, cols).start()
            put(h, cols).wait()
            return unused

        lax.fori_loop(0, GROUP, exact_head, 0)


def own_pair_seen():
    y, z, x, core = coordinates()
    row_at = lax.broadcasted_iota(jnp.int32, (SUB, ROWS), 1) + z // 2 * ROWS
    key_at = lax.broadcasted_iota(jnp.int32, (SUB, ROWS), 0)
    for i, z_step in enumerate(STEPS):
        for j, x_step in enumerate(STEPS):
            x0, z0 = (x - x_step) % 4, (z - z_step) % 4
            for lane in range(2):
                first = (z0 // 2) * ROWS + ((x0 * 2 + z0 % 2) * 2 + 1 - lane) * SUB
                at = ((i * 4 + j) * 2 + lane) * SUB
                yield slice(at, at + SUB), key_at + first <= row_at


def here_kernel(q_ref, q_rows, acc_in, sum_in, here, other, *refs):
    acc_ref, sum_ref, acc_rows, sum_rows, kb, vt, kb_rows, vt_rows, seen = refs
    load_chunk(0, here, other, kb, vt)
    load_chunk(1, here, other, kb_rows, vt_rows)
    for pair in range(0, GROUP, 2):
        for h, sums, accs in weigh_pair(kb[...], q_ref, pair, vt[...]):
            sum_ref[h] = sum_in[h] + sums
            acc_ref[h] = acc_in[h] + accs

    for rows, visible in own_pair_seen():
        seen[rows, :] = jnp.where(visible, 0.0, -jnp.inf)
    for pair in range(0, HALF_HEADS, 2):
        for h, sums, accs in weigh_pair(kb_rows[...], q_rows, pair, vt_rows[...], seen[...]):
            sum_rows[h], acc_rows[h] = sums, accs


HALF_HEADS = GROUP // 2
PAIR = 2 * ROWS
CHUNK = jax.ShapeDtypeStruct((8, 2, HD, HD), jnp.bfloat16)


def state_of(heads):
    return (
        jax.ShapeDtypeStruct((heads, HD, ROWS), jnp.float32),
        jax.ShapeDtypeStruct((heads, 8, ROWS), jnp.float32),
    )


SCALAR = pl.BlockSpec(memory_space=pltpu.SMEM)
VMEM = pl.BlockSpec(memory_space=pltpu.VMEM)
ANYWHERE = pl.BlockSpec(memory_space=pl.ANY)


def keys_of(count):
    return [pltpu.VMEM((count, HD), jnp.bfloat16), pltpu.VMEM((HD, count), jnp.bfloat16)]


KEYS = keys_of(PAIR)


def call(kernel, name, in_specs, out_shape, scratch, rows, keys, out=VMEM):
    single = not isinstance(out_shape, tuple)
    return pl.pallas_call(
        kernel,
        in_specs=in_specs,
        out_specs=out if single else tuple(out for _ in out_shape),
        out_shape=out_shape,
        scratch_shapes=scratch,
        cost_estimate=pl.CostEstimate(
            flops=8 * rows * keys * HD, bytes_accessed=6 * MIB, transcendentals=rows * keys
        ),
        compiler_params=pltpu.CompilerParams(vmem_limit_bytes=32 * MIB),
        name=name,
    )


def attend_own(tree, length, q, k, v):
    scratch = [pltpu.VMEM((HD, ROWS), jnp.bfloat16)]
    specs = [SCALAR, SCALAR, VMEM, VMEM, VMEM]
    out = state_of(GROUP) + (
        jax.ShapeDtypeStruct((ROWS, ROWS), jnp.float32),
        jax.ShapeDtypeStruct((8, ROWS), jnp.float32),
    )
    outs = call(own_kernel, "own_keys", specs, out, scratch, GROUP * ROWS, ROWS)(
        tree, length, q, k, v
    )
    return outs[:2], outs[2], outs[3]


def pick(own, k_other, v_other):
    out = tuple(jax.ShapeDtypeStruct((2, 2 * SUB, 2 * HD), jnp.bfloat16) for _ in STEPS)
    return call(pick_kernel, "pick", [VMEM] * 3, out, [], 8, 8)(own, k_other, v_other)


def arrange(parts):
    return call(arrange_kernel, "arrange", [VMEM] * 4, CHUNK, [], 8, 8)(*parts)


def attend_here(q, q_rows, state, here, other):
    scratch = KEYS + KEYS + [pltpu.VMEM((PAIR, ROWS), jnp.float32)]
    out = state_of(GROUP) + state_of(HALF_HEADS)
    outs = call(here_kernel, "here_keys", [VMEM] * 6, out, scratch, 3 * HALF_HEADS * ROWS, PAIR)(
        q, q_rows, *state, here, other
    )
    return outs[:2], outs[2:]


def attend_sides(kernel, name, heads, q, state, sides):
    scratch = keys_of(2 * PAIR)
    return call(kernel, name, [VMEM] * 7, state_of(heads), scratch, heads * ROWS, 2 * PAIR)(
        q, *state, *sides
    )


def attend_last(q, state, live, q_rows, state_rows, held, k_own, v_own, seen):
    specs = [VMEM] * (7 + len(held)) + [ANYWHERE] * (3 + len(held))
    scratch = [
        pltpu.VMEM((ROWS, GROUP * HD), jnp.bfloat16),
        pltpu.VMEM(q_rows.shape, jnp.bfloat16),
        pltpu.SemaphoreType.DMA((GROUP + 1,)),
    ]
    scratch += KEYS + [
        pltpu.VMEM((1, ROWS), jnp.float32),
        pltpu.VMEM((1, ROWS), jnp.float32),
        pltpu.VMEM((2, HD, HD), jnp.bfloat16),
        pltpu.VMEM((2, ROWS, HD), jnp.bfloat16),
    ]
    scratch += KEYS + [
        pltpu.VMEM((PAIR, ROWS), jnp.float32),
        pltpu.VMEM((HALF_HEADS, HD, ROWS), jnp.float32),
        pltpu.VMEM((HALF_HEADS, 8, ROWS), jnp.float32),
        pltpu.VMEM((HALF_HEADS, 1, ROWS), jnp.float32),
    ]
    out = (
        jax.ShapeDtypeStruct((ROWS, GROUP * HD), jnp.bfloat16),
        jax.ShapeDtypeStruct(q_rows.shape, jnp.bfloat16),
    )
    return call(last_kernel, "last_keys", specs, out, scratch, 2 * GROUP * ROWS, PAIR, ANYWHERE)(
        q, *state, live, q_rows, *state_rows, *held, k_own, v_own, seen, *held
    )


def after(value, *events):
    return lax.optimization_barrier((value, *events))[0]


def on_device(q_prompt, k_prompt, v_prompt, q_resp, k_resp, v_resp, tree_table, lengths):
    y, z, x, core = coordinates()
    q = q_resp[0]

    def cols(block, at, count):
        return lax.dynamic_slice_in_dim(block, at * count * HD, count * HD, block.ndim - 1)

    own = jnp.stack([k_prompt, v_prompt])
    over = pick(own, move(k_prompt, other_core), move(v_prompt, other_core))
    over = [over[0]] + [move(part, first_axis(d)) for part, d in zip(over[1:], STEPS[1:])]
    over = jnp.stack(over)

    def for_z(at):
        return cols(over, jnp.where(core == 0, at // 2, at % 2), 1)

    over_z = [for_z(z)] + [move(for_z((z + d) % 4), along_z(d)) for d in STEPS[1:]]
    q = after(q, over)
    state, seen, live = attend_own(tree_table, lengths, q, k_resp[0], v_resp[0])
    over_z = after(over_z, live)
    here = arrange(over_z)
    here_o = move(here, other_core)
    left, right = move(here, last_axis(1)), move(here, last_axis(3))
    state, rows_state = attend_here(q, q_prompt, state, here, here_o)
    left, right = after((left, right), state[1])
    left_o, right_o = move(left, other_core), move(right, other_core)
    far = move(left, last_axis(1))
    sides = (left, left_o, right, right_o)
    state = attend_sides(wide_kernel, "wide_keys", GROUP, q, state, sides)
    far = after(far, state[1])
    far_o = move(far, other_core)
    rows_state = attend_sides(side_kernel, "side_rows", HALF_HEADS, q_prompt, rows_state, sides)
    held = (here, left, right, far, here_o, left_o, right_o, after(far_o, rows_state[1]))
    resp_out, prompt_out = attend_last(
        q, state, live, q_prompt, rows_state, held, k_resp[0], v_resp[0], seen
    )
    return (prompt_out, resp_out[None])


def solution(mesh):
    placed = (
        P("chain", "resp"),
        P(("chain", "resp"), None),
        P(("chain", "resp"), None),
        P("resp", None, "chain"),
        P("resp", None, "chain"),
        P("resp", None, "chain"),
        P("resp", None),
        P("resp"),
    )
    return jax.shard_map(
        on_device,
        mesh=mesh,
        in_specs=placed,
        out_specs=(P("chain", "resp"), P("resp", None, "chain")),
        check_vma=False,
    )
```

```python
import functools

import jax
import jax.numpy as jnp
from jax import lax
from jax.experimental import pallas as pl
from jax.experimental.pallas import tpu as pltpu
from jax.sharding import PartitionSpec as P

QH = 64
KVH = 8
HD = 128
RBLK = 8
ROWS = 512
SUB = 32
GROUP = QH // KVH
STEP_HEADS = 4
SCALE = HD**-0.5 * 1.4426950408889634
LOW, HIGH = 1e-18, 1e30
AXES = ("chain", "resp")
STEPS = (0, 1, 3, 2)
CHUNKS = 4
MIB = 2**20
PLACES = [(y, z, x, k) for y in range(4) for z in range(4) for x in range(4) for k in range(2)]


def device_at(y, z, x, core):
    return (y * 2 + z // 2) * 16 + (x * 2 + z % 2) * 2 + core


def move(block, target):
    route = [(device_at(*p), device_at(*target(*p))) for p in PLACES]
    return lax.ppermute(block, AXES, route)


def first_axis(d):
    def target(y, z, x, core):
        return (y, z, (x + d) % 4, core) if core else ((y + d) % 4, z, x, core)

    return target


def along_z(d):
    return lambda y, z, x, core: (y, (z + d) % 4, x, core)


def last_axis(d):
    def target(y, z, x, core):
        return ((y + d) % 4, z, x, core) if core else (y, z, (x + d) % 4, core)

    return target


def other_core(y, z, x, core):
    return (y, z, x, 1 - core)


def coordinates():
    chain, resp = lax.axis_index("chain"), lax.axis_index("resp")
    return chain // 2, chain % 2 * 2 + resp // 2 % 2, resp // 4, resp % 2


def dot_t(a, b):
    return lax.dot_general(a, b, (((1,), (1,)), ((), ())), preferred_element_type=jnp.float32)


def fold_rows(p):
    return jnp.sum(p.reshape(p.shape[0] // 8, 8, p.shape[1]), axis=0)


def online(carried, keys, values_t, queries, visible):
    run_max, run_sum, run_acc = carried
    scores = dot_t(keys, queries) * SCALE
    if visible is not None:
        scores = jnp.where(visible, scores, -1e30)
    new_max = jnp.maximum(run_max, jnp.max(scores, axis=0, keepdims=True))
    weights = jnp.exp2(scores - new_max)
    if visible is not None:
        weights = jnp.where(visible, weights, 0.0)
    rescale = jnp.exp2(run_max - new_max)
    run_sum = run_sum * rescale + jnp.sum(weights, axis=0, keepdims=True)
    added = jnp.dot(values_t, weights.astype(jnp.bfloat16), preferred_element_type=jnp.float32)
    return (new_max, run_sum, run_acc * rescale + added)


def fresh(cols):
    return (
        jnp.full((1, cols), -1e30, jnp.float32),
        jnp.zeros((1, cols), jnp.float32),
        jnp.zeros((HD, cols), jnp.float32),
    )


def tree_seen(tree_ref, len_ref):
    lines = []
    for j in range(RBLK):
        parent = tree_ref[0, j]
        line = jnp.int32(1 << j)
        for i in range(j):
            line = line | jnp.where(parent == i, lines[i], 0)
        lines.append(line)
    key_at = lax.broadcasted_iota(jnp.int32, (ROWS, ROWS), 0)
    row_at = lax.broadcasted_iota(jnp.int32, (ROWS, ROWS), 1)
    span = ROWS // RBLK
    line_of_row = jnp.zeros((ROWS, ROWS), jnp.int32)
    for j in range(RBLK):
        line_of_row = jnp.where(row_at // span == j, lines[j], line_of_row)
    related = (lax.shift_right_logical(line_of_row, key_at // span) & 1) == 1
    return related & (key_at <= row_at) & (key_at < len_ref[0])


def weigh(keys, queries, values_t, shown=None):
    scores = dot_t(keys, queries) * SCALE
    weights = jnp.exp2(scores if shown is None else scores + shown)
    added = jnp.dot(values_t, weights.astype(jnp.bfloat16), preferred_element_type=jnp.float32)
    return fold_rows(weights), added


def weigh_pair(keys, q_ref, h, values_t, shown=None):
    queries = jnp.concatenate([q_ref[:, (h + i) * HD : (h + i + 1) * HD] for i in range(2)])
    if shown is not None:
        shown = jnp.concatenate([shown, shown], 1)
    sums, accs = weigh(keys, queries, values_t, shown)
    for i in range(2):
        yield h + i, sums[:, i * ROWS : (i + 1) * ROWS], accs[:, i * ROWS : (i + 1) * ROWS]


def over_heads(one_head):
    def some(step, unused):
        for h in range(STEP_HEADS):
            head = step * STEP_HEADS + h
            one_head(head, pl.ds(pl.multiple_of(head * HD, HD), HD))
        return unused

    lax.fori_loop(0, GROUP // STEP_HEADS, some, 0)


def own_kernel(tree_ref, len_ref, q_ref, k_ref, v_ref, acc_ref, sum_ref, seen, live, vt):
    vt[...] = v_ref[...].T
    rows = lax.broadcasted_iota(jnp.int32, live.shape, 1)
    live[...] = jnp.where(rows < len_ref[0], 1.0, 0.0)
    seen[...] = jnp.where(tree_seen(tree_ref, len_ref), 0.0, -jnp.inf)

    def one_head(h, cols):
        sum_ref[h], acc_ref[h] = weigh(k_ref[...], q_ref[:, cols], vt[...], seen[...])

    over_heads(one_head)


def pick_kernel(own, k_other, v_other, *outs):
    y, z, x, core = coordinates()
    near = jnp.where(core == 0, y, x)
    for step, out_ref in zip(STEPS, outs):
        width = 2 * HD
        cols = pl.ds(pl.multiple_of((near + step) % 4 * width, width), width)
        for i, other in enumerate((k_other, v_other)):
            out_ref[i, :SUB, :] = own[i, :, cols]
            out_ref[i, SUB:, :] = other[:, cols]


def arrange_kernel(*refs):
    out_ref = refs[4]
    for i, ref in enumerate(refs[:4]):
        for half in range(2):
            pieces = ref[2 * half : 2 * half + 2]
            out_ref[2 * i + half, 0] = pieces[:, 0].reshape(HD, HD)
            out_ref[2 * i + half, 1] = pieces[:, 1].reshape(HD, HD).T


def load_blocks(chunk, kb, vt):
    for b in range(8):
        kb[b * HD : (b + 1) * HD, :] = chunk[b, 0]
        vt[:, b * HD : (b + 1) * HD] = chunk[b, 1]


def load_chunk(role, here, other, kb, vt):
    core = coordinates()[3]

    @pl.when(core == role)
    def _():
        load_blocks(here, kb, vt)

    @pl.when(core != role)
    def _():
        load_blocks(other, kb, vt)


def load_sides(role, left, left_o, right, right_o, kb, vt):
    load_chunk(role, left, left_o, kb.at[:PAIR], vt.at[:, :PAIR])
    load_chunk(role, right, right_o, kb.at[PAIR:], vt.at[:, PAIR:])


def wide_kernel(q_ref, acc_in, sum_in, left, left_o, right, right_o, acc_ref, sum_ref, kb, vt):
    load_sides(0, left, left_o, right, right_o, kb, vt)
    add_heads(q_ref, acc_in, sum_in, acc_ref, sum_ref, kb, vt)


def add_heads(q_ref, acc_in, sum_in, acc_ref, sum_ref, kb, vt):
    def one_head(h, cols):
        sums, accs = weigh(kb[...], q_ref[:, cols], vt[...])
        sum_ref[h] = sum_in[h] + sums
        acc_ref[h] = acc_in[h] + accs

    over_heads(one_head)


def in_range(low, high):
    return (jnp.min(low) > LOW) & (jnp.max(high) < HIGH)


def side_kernel(q_ref, acc_in, sum_in, left, left_o, right, right_o, acc_ref, sum_ref, kb, vt):
    y = coordinates()[0]
    load_sides(1, left, left_o, right, right_o, kb, vt)

    def add(count):
        for h in range(HALF_HEADS):
            queries = q_ref[:, h * HD : (h + 1) * HD]
            sums, accs = weigh(kb[:count], queries, vt[:, :count])
            sum_ref[h] = sum_in[h] + sums
            acc_ref[h] = acc_in[h] + accs

    @pl.when(y == 3)
    def _():
        add(2 * PAIR)

    @pl.when((y == 1) | (y == 2))
    def _():
        add(PAIR)

    @pl.when(y == 0)
    def _():
        sum_ref[...] = sum_in[...]
        acc_ref[...] = acc_in[...]


def prompt_part(q_ref, acc_in, sum_in, held, out_ref, put, kb, vt, seen, acc, total, top):
    y = coordinates()[0]

    def queries(h):
        return q_ref[:, h * HD : (h + 1) * HD]

    @pl.when(y >= 2)
    def _():
        load_chunk(1, held[3], held[CHUNKS + 3], kb, vt)
        for pair in range(0, HALF_HEADS, 2):
            for h, sums, accs in weigh_pair(kb[...], q_ref, pair, vt[...]):
                total[h] = sum_in[h] + sums
                acc[h] = acc_in[h] + accs

    @pl.when(y < 2)
    def _():
        total[...] = sum_in[...]
        acc[...] = acc_in[...]

    def store(h, sums):
        shown = (acc[h] * (1.0 / sums)).astype(jnp.bfloat16)
        out_ref[:, h * HD : (h + 1) * HD] = shown.T

    low = high = jnp.ones((1, ROWS), jnp.float32)
    for h in range(HALF_HEADS):
        sums = jnp.sum(total[h], axis=0, keepdims=True)
        store(h, sums)
        low, high = jnp.minimum(low, sums), jnp.maximum(high, sums)
    put.start()

    def exact_rows():
        load_chunk(1, held[0], held[CHUNKS], kb, vt)
        for rows, visible in own_pair_seen():
            seen[rows, :] = jnp.where(visible, 1.0, 0.0)
        top[...] = jnp.full_like(top, -1e30)
        total[...] = jnp.zeros_like(total)
        acc[...] = jnp.zeros_like(acc)

        def exact():
            def one_head(h, unused):
                cols = pl.ds(pl.multiple_of(h * HD, HD), HD)
                carried = (top[h], total[h, 0:1], acc[h])
                carried = online(carried, kb[...], vt[...], q_ref[:, cols], seen[...] > 0.5)
                top[h], total[h, 0:1], acc[h] = carried
                return unused

            lax.fori_loop(0, HALF_HEADS, one_head, 0)

        exact()
        seen[...] = jnp.ones_like(seen)

        def one_pair(i, unused):
            for at, spot in enumerate((1, 3, 2)):

                @pl.when(i == at)
                def _(spot=spot):
                    load_chunk(1, held[spot], held[CHUNKS + spot], kb, vt)

            exact()
            return unused

        lax.fori_loop(0, y, one_pair, 0)
        for h in range(HALF_HEADS):
            store(h, total[h, 0:1])
        put.start()
        put.wait()

    return low, high, exact_rows


def last_kernel(q_ref, acc_in, sum_in, live_ref, *refs):
    q_rows, acc_rows, sum_rows = refs[:3]
    rows_held, (k_own, v_own, seen_own), refs = refs[3 : 3 + 2 * CHUNKS], refs[11:14], refs[14:]
    held, refs = refs[: 2 * CHUNKS], refs[2 * CHUNKS :]
    out_hbm, rows_hbm, out_ref, out_rows, done, kb, vt, low, high, block, own = refs[:11]
    put_rows = pltpu.make_async_copy(out_rows, rows_hbm, done.at[GROUP])
    low[...], high[...], exact_rows = prompt_part(
        q_rows, acc_rows, sum_rows, rows_held, out_rows, put_rows, *refs[11:]
    )

    def put(h, cols):
        return pltpu.make_async_copy(out_ref.at[:, cols], out_hbm.at[:, cols], done.at[h])

    is_first = coordinates()[3] == 0
    load_chunk(0, rows_held[CHUNKS - 1], rows_held[2 * CHUNKS - 1], kb, vt)
    live = live_ref[0:1] > 0.5

    def store(cols, acc, total):
        shown = jnp.where(live, acc * (1.0 / total), 0.0)
        out_ref[:, cols] = shown.astype(jnp.bfloat16).T

    for pair in range(0, GROUP, 2):
        for h, sums, accs in weigh_pair(kb[...], q_ref, pair, vt[...]):
            total = jnp.sum(sum_in[h] + sums, axis=0, keepdims=True)
            low[...] = jnp.minimum(low[...], total)
            high[...] = jnp.maximum(high[...], total)
            cols = slice(h * HD, (h + 1) * HD)
            store(cols, acc_in[h] + accs, total)
            put(h, cols).start()
    good = in_range(low[...], high[...])
    put_rows.wait()
    for h in range(GROUP):
        put(h, slice(h * HD, (h + 1) * HD)).wait()

    @pl.when(jnp.logical_not(good))
    def _():
        pltpu.sync_copy(k_own, own.at[0])
        pltpu.sync_copy(v_own, own.at[1])
        exact_rows()
        seen_buf = refs[13].at[:ROWS]
        pltpu.sync_copy(seen_own, seen_buf)

        def exact_head(h, unused):
            cols = pl.ds(pl.multiple_of(h * HD, HD), HD)
            queries = q_ref[:, cols]

            def one_block(i, carried, one, two):
                @pl.when(is_first)
                def _():
                    pltpu.sync_copy(one.at[i], block)

                @pl.when(jnp.logical_not(is_first))
                def _():
                    pltpu.sync_copy(two.at[i], block)

                return online(carried, block[0], block[1], queries, None)

            carried = fresh(ROWS)
            for one, two in zip(held[:CHUNKS], held[CHUNKS:]):
                carried = lax.fori_loop(
                    0, 8, functools.partial(one_block, one=one, two=two), carried
                )
            visible = seen_buf[...] > -1.0
            run_max, run_sum, run_acc = online(carried, own[0], own[1].T, queries, visible)
            store(cols, run_acc, run_sum)
            put(h, cols).start()
            put(h, cols).wait()
            return unused

        lax.fori_loop(0, GROUP, exact_head, 0)


def own_pair_seen():
    y, z, x, core = coordinates()
    row_at = lax.broadcasted_iota(jnp.int32, (SUB, ROWS), 1) + z // 2 * ROWS
    key_at = lax.broadcasted_iota(jnp.int32, (SUB, ROWS), 0)
    for i, z_step in enumerate(STEPS):
        for j, x_step in enumerate(STEPS):
            x0, z0 = (x - x_step) % 4, (z - z_step) % 4
            for lane in range(2):
                first = (z0 // 2) * ROWS + ((x0 * 2 + z0 % 2) * 2 + 1 - lane) * SUB
                at = ((i * 4 + j) * 2 + lane) * SUB
                yield slice(at, at + SUB), key_at + first <= row_at


def here_kernel(q_ref, q_rows, acc_in, sum_in, here, other, *refs):
    acc_ref, sum_ref, acc_rows, sum_rows, kb, vt, kb_rows, vt_rows, seen = refs
    load_chunk(0, here, other, kb, vt)
    load_chunk(1, here, other, kb_rows, vt_rows)
    for pair in range(0, GROUP, 2):
        for h, sums, accs in weigh_pair(kb[...], q_ref, pair, vt[...]):
            sum_ref[h] = sum_in[h] + sums
            acc_ref[h] = acc_in[h] + accs

    for rows, visible in own_pair_seen():
        seen[rows, :] = jnp.where(visible, 0.0, -jnp.inf)
    for pair in range(0, HALF_HEADS, 2):
        for h, sums, accs in weigh_pair(kb_rows[...], q_rows, pair, vt_rows[...], seen[...]):
            sum_rows[h], acc_rows[h] = sums, accs


HALF_HEADS = GROUP // 2
PAIR = 2 * ROWS
CHUNK = jax.ShapeDtypeStruct((8, 2, HD, HD), jnp.bfloat16)


def state_of(heads):
    return (
        jax.ShapeDtypeStruct((heads, HD, ROWS), jnp.float32),
        jax.ShapeDtypeStruct((heads, 8, ROWS), jnp.float32),
    )


SCALAR = pl.BlockSpec(memory_space=pltpu.SMEM)
VMEM = pl.BlockSpec(memory_space=pltpu.VMEM)
ANYWHERE = pl.BlockSpec(memory_space=pl.ANY)


def keys_of(count):
    return [pltpu.VMEM((count, HD), jnp.bfloat16), pltpu.VMEM((HD, count), jnp.bfloat16)]


KEYS = keys_of(PAIR)


def call(kernel, name, in_specs, out_shape, scratch, rows, keys, out=VMEM):
    single = not isinstance(out_shape, tuple)
    return pl.pallas_call(
        kernel,
        in_specs=in_specs,
        out_specs=out if single else tuple(out for _ in out_shape),
        out_shape=out_shape,
        scratch_shapes=scratch,
        cost_estimate=pl.CostEstimate(
            flops=8 * rows * keys * HD, bytes_accessed=6 * MIB, transcendentals=rows * keys
        ),
        compiler_params=pltpu.CompilerParams(vmem_limit_bytes=32 * MIB),
        name=name,
    )


def attend_own(tree, length, q, k, v):
    scratch = [pltpu.VMEM((HD, ROWS), jnp.bfloat16)]
    specs = [SCALAR, SCALAR, VMEM, VMEM, VMEM]
    out = state_of(GROUP) + (
        jax.ShapeDtypeStruct((ROWS, ROWS), jnp.float32),
        jax.ShapeDtypeStruct((8, ROWS), jnp.float32),
    )
    outs = call(own_kernel, "own_keys", specs, out, scratch, GROUP * ROWS, ROWS)(
        tree, length, q, k, v
    )
    return outs[:2], outs[2], outs[3]


def pick(own, k_other, v_other):
    out = tuple(jax.ShapeDtypeStruct((2, 2 * SUB, 2 * HD), jnp.bfloat16) for _ in STEPS)
    return call(pick_kernel, "pick", [VMEM] * 3, out, [], 8, 8)(own, k_other, v_other)


def arrange(parts):
    return call(arrange_kernel, "arrange", [VMEM] * 4, CHUNK, [], 8, 8)(*parts)


def attend_here(q, q_rows, state, here, other):
    scratch = KEYS + KEYS + [pltpu.VMEM((PAIR, ROWS), jnp.float32)]
    out = state_of(GROUP) + state_of(HALF_HEADS)
    outs = call(here_kernel, "here_keys", [VMEM] * 6, out, scratch, 8, 8)(
        q, q_rows, *state, here, other
    )
    return outs[:2], outs[2:]


def attend_sides(kernel, name, heads, q, state, sides):
    scratch = keys_of(2 * PAIR)
    return call(kernel, name, [VMEM] * 7, state_of(heads), scratch, heads * ROWS, 2 * PAIR)(
        q, *state, *sides
    )


def attend_last(q, state, live, q_rows, state_rows, held, k_own, v_own, seen):
    specs = [VMEM] * (7 + len(held)) + [ANYWHERE] * (3 + len(held))
    scratch = [
        pltpu.VMEM((ROWS, GROUP * HD), jnp.bfloat16),
        pltpu.VMEM(q_rows.shape, jnp.bfloat16),
        pltpu.SemaphoreType.DMA((GROUP + 1,)),
    ]
    scratch += KEYS + [
        pltpu.VMEM((1, ROWS), jnp.float32),
        pltpu.VMEM((1, ROWS), jnp.float32),
        pltpu.VMEM((2, HD, HD), jnp.bfloat16),
        pltpu.VMEM((2, ROWS, HD), jnp.bfloat16),
    ]
    scratch += KEYS + [
        pltpu.VMEM((PAIR, ROWS), jnp.float32),
        pltpu.VMEM((HALF_HEADS, HD, ROWS), jnp.float32),
        pltpu.VMEM((HALF_HEADS, 8, ROWS), jnp.float32),
        pltpu.VMEM((HALF_HEADS, 1, ROWS), jnp.float32),
    ]
    out = (
        jax.ShapeDtypeStruct((ROWS, GROUP * HD), jnp.bfloat16),
        jax.ShapeDtypeStruct(q_rows.shape, jnp.bfloat16),
    )
    return call(last_kernel, "last_keys", specs, out, scratch, 2 * GROUP * ROWS, PAIR, ANYWHERE)(
        q, *state, live, q_rows, *state_rows, *held, k_own, v_own, seen, *held
    )


def after(value, *events):
    return lax.optimization_barrier((value, *events))[0]


def on_device(q_prompt, k_prompt, v_prompt, q_resp, k_resp, v_resp, tree_table, lengths):
    y, z, x, core = coordinates()
    q = q_resp[0]

    def cols(block, at, count):
        return lax.dynamic_slice_in_dim(block, at * count * HD, count * HD, block.ndim - 1)

    own = jnp.stack([k_prompt, v_prompt])
    over = pick(own, move(k_prompt, other_core), move(v_prompt, other_core))
    over = [over[0]] + [move(part, first_axis(d)) for part, d in zip(over[1:], STEPS[1:])]
    over = jnp.stack(over)

    def for_z(at):
        return cols(over, jnp.where(core == 0, at // 2, at % 2), 1)

    over_z = [for_z(z)] + [move(for_z((z + d) % 4), along_z(d)) for d in STEPS[1:]]
    q = after(q, over)
    state, seen, live = attend_own(tree_table, lengths, q, k_resp[0], v_resp[0])
    over_z = after(over_z, live)
    here = arrange(over_z)
    here_o = move(here, other_core)
    left, right = move(here, last_axis(1)), move(here, last_axis(3))
    state, rows_state = attend_here(q, q_prompt, state, here, here_o)
    left, right = after((left, right), state[1])
    left_o, right_o = move(left, other_core), move(right, other_core)
    far = move(left, last_axis(1))
    sides = (left, left_o, right, right_o)
    state = attend_sides(wide_kernel, "wide_keys", GROUP, q, state, sides)
    far = after(far, state[1])
    far_o = move(far, other_core)
    rows_state = attend_sides(side_kernel, "side_rows", HALF_HEADS, q_prompt, rows_state, sides)
    held = (here, left, right, far, here_o, left_o, right_o, after(far_o, rows_state[1]))
    resp_out, prompt_out = attend_last(
        q, state, live, q_prompt, rows_state, held, k_resp[0], v_resp[0], seen
    )
    return (prompt_out, resp_out[None])


def solution(mesh):
    placed = (
        P("chain", "resp"),
        P(("chain", "resp"), None),
        P(("chain", "resp"), None),
        P("resp", None, "chain"),
        P("resp", None, "chain"),
        P("resp", None, "chain"),
        P("resp", None),
        P("resp"),
    )
    return jax.shard_map(
        on_device,
        mesh=mesh,
        in_specs=placed,
        out_specs=(P("chain", "resp"), P("resp", None, "chain")),
        check_vma=False,
    )
```
